32 devices in a mesh: group: 4 (over y, x), dom: 8 (over z, core).
Axes of the slice: x: 2, y: 2, z: 4, core: 2. Of those that a mesh axis runs over, the one named last changes fastest.
Arguments:
- density: float32 [64, 16384], P(None, ('group', 'dom')), may hold values from 0.8 to 1.2
- momentum: float32 [3, 64, 16384], P(None, None, ('group', 'dom')), may hold values from -0.5 to 0.5
- energy: float32 [64, 16384], P(None, ('group', 'dom')), may hold values from 2.5 to 3.5
- face_link: int32 [4, 8, 3072], P('group', 'dom'), may hold values from 0 to 3455, as said below
- owner_rank: int32 [4096, 1], P(('group', 'dom')), may hold values from 0 to 7; in each aligned block of 128 rows (0 to 127, 128 to 255, ...) at most 32 rows name the same one
- owner_element: int32 [4, 4096], P(None, ('group', 'dom')), may hold values from 0 to 511
- point_offset: float32 [3, 4, 4096], P(None, None, ('group', 'dom')), may hold values from -1.5 to 1.5
- point_force: float32 [3, 4096], P(None, ('group', 'dom')), may hold values from -4 to 4
Outputs:
- new_density: float32 [64, 16384], P(None, ('group', 'dom'))
- new_momentum: float32 [3, 64, 16384], P(None, None, ('group', 'dom'))
- new_energy: float32 [64, 16384], P(None, ('group', 'dom'))
- tendency: float32 [5, 64, 16384], P(None, None, ('group', 'dom'))
The draws below stay inside these ranges and needn't reach their ends.
Inputs may be any that keep to these rules, and one draw needn't show every extreme that they name: `face_link`: on each device the values are all different; every value from 3072 up appears exactly once, and a value v below 3072 on face f means that face v has the value f: faces within a device are paired. `owner_rank`: in the 128 rows of one device no value appears more than 32 times, and in every draw some device names some value exactly 32 times.
All inputs are finite; a program needn't handle non-finite values.
Results may differ from the reference program's by a relative error of at most 0.0003.
Values sent between devices are 32-bit elements; how exact they have to be, the bound alone decides.
A program may use at most 64 MiB of HBM per device.

```python
import math
import jax
import jax.numpy as jnp
import numpy as np
from jax import lax

NODES = 64
E_DEV = 512
SF = 16
GF = 128
P_DEV = 128
K_OWN = 4
CAP = 32
ELEMS = 16384
POINTS = 4096
N_GROUP = 4
N_DOM = 8


def draw_face_link(key, part):
    key = jax.random.fold_in(key, 11)
    faces = 6 * E_DEV
    remote = N_DOM * SF + 2 * GF
    devices = N_GROUP * N_DOM
    keys = jax.random.split(key, devices)
    ordering = jax.vmap(lambda k: jax.random.permutation(k, faces))(keys).astype(jnp.int32)
    position = jnp.arange(faces, dtype=jnp.int32)
    partner_position = jnp.where(position < remote, position, remote + jnp.bitwise_xor(position - remote, 1))
    partner = jnp.take_along_axis(ordering, jnp.broadcast_to(partner_position[None, :], ordering.shape), axis=1)
    target = jnp.where(position[None, :] < remote, faces + position[None, :], partner)
    device_rows = jnp.broadcast_to(jnp.arange(devices, dtype=jnp.int32)[:, None], ordering.shape)
    result = jnp.zeros((devices, faces), jnp.int32).at[device_rows, ordering].set(target)
    return result.reshape(N_GROUP, N_DOM, faces)


def with_ends(drawn, rng, smallest, high):
    index_at = [jax.random.randint(jax.random.fold_in(rng, axis), (), 0, length) for axis, length in enumerate(drawn.shape)]
    widest = drawn.shape.index(max(drawn.shape))
    beside = index_at[:widest] + [(index_at[widest] + 1) % drawn.shape[widest]] + index_at[widest + 1:]
    return drawn.at[tuple(index_at)].set(smallest).at[tuple(beside)].set(high)


def shard_levels(own_key, dims, cuts, least, high):
    def one(dim, blocks):
        draws = jax.random.uniform(jax.random.fold_in(jax.random.fold_in(own_key, 6), dim), (blocks,), jnp.float32, least / len(cuts), high / len(cuts))
        return jnp.repeat(jnp.exp(draws), dims[dim] // blocks).reshape((-1,) + (1,) * (len(dims) - dim - 1))

    loudness = one(*cuts[0])
    for cut in cuts[1:]:
        loudness = loudness * one(*cut)
    return loudness


def assign_block(own_key, own, number, rows, amount, top, bound, lean):
    sequence = jax.random.permutation(own_key, amount)
    heavy_load, ordinary = portions_of(amount, rows * top, bound, lean, True), portions_of(amount, rows * top, bound, lean, False)
    places = jnp.arange(amount)

    def named(sizes, offset_by):
        used = int((sizes > 0).sum())
        fixed = max(1, used // 4)
        passed = fixed + (places - fixed + offset_by * (used - fixed)) % max(1, amount - fixed)
        return jnp.zeros((amount,), jnp.int32).at[sequence[jnp.where(places < fixed, places, passed)]].set(jnp.asarray(sizes, jnp.int32))

    sizes = jnp.where(number % 4 == 0, named(heavy_load, number // 4), named(ordinary, number - number // 4 - 1))
    mixed = jax.random.permutation(jax.random.fold_in(own, 3), amount)
    donor, sink = mixed[0:amount // 2 * 2:2], mixed[1:amount // 2 * 2:2]
    slack = jnp.minimum(sizes[donor] - 1, bound - sizes[sink]) // 2
    slack = jnp.where((donor == sequence[0]) | (sink == sequence[0]) | (sizes[sink] == 0), 0, jnp.maximum(slack, 0))
    passed = jax.random.randint(jax.random.fold_in(own, 4), (amount // 2,), 0, 1 << 20) % (slack + 1)
    sizes = sizes.at[donor].add(-passed).at[sink].add(passed)
    members = jnp.searchsorted(jnp.cumsum(sizes), jnp.arange(rows * top), side="right").astype(jnp.int32)
    table = members.reshape(top, rows).T
    table = table[jax.random.permutation(jax.random.fold_in(own, 1), rows)]
    offset_by = jax.random.randint(jax.random.fold_in(own, 2), (rows, 1), 0, top)
    return jnp.take_along_axis(table, (jnp.arange(top)[None, :] + offset_by) % top, axis=1)


def portions_of(count, total, limit, skew, full):
    portions = [(1 << 20) // math.isqrt(grade ** skew) + 1 for grade in range(1, count + 1)]
    largest = limit if full else min(limit, max(-(-total // count), total * portions[0] // sum(portions)))
    least = 1 if total - largest >= count - 1 else 0
    counts, surplus = [largest] + [least] * (count - 1), total - largest - least * (count - 1)
    while surplus > 0:
        candidates = [i for i in range(1, count) if counts[i] < largest] or [i for i in range(1, count) if counts[i] < limit]
        pool, left = sum([portions[i] for i in candidates]), surplus
        for i in candidates:
            addition = min(limit - counts[i], max(1, left * portions[i] // pool), surplus)
            counts[i] = counts[i] + addition
            surplus = surplus - addition
    return np.array(counts)


def centred(rng, shape, width, limit, cuts=(), held_as=jnp.bfloat16):
    values = width * jax.random.normal(rng, shape, jnp.float32)
    if cuts:
        values = values * shard_levels(rng, shape, cuts, -0.22, 0.18)
    return jnp.clip(values, -limit, limit).astype(held_as)


def setup_inputs(seed: int = 0) -> dict:
    key_list = jax.random.split(jax.random.key(seed), 9)
    density = jnp.clip(0.8 + 0.40000004 * jax.random.uniform(key_list[0], (NODES, ELEMS), jnp.float32) ** shard_levels(key_list[0], (NODES, ELEMS), ((1, 32),), -0.2, 0.2), 0.8, 1.2)
    momentum = jnp.clip(jax.random.uniform(key_list[1], (3, NODES, ELEMS), jnp.float32, -0.5, 0.5) * shard_levels(key_list[1], (3, NODES, ELEMS), ((2, 32),), -0.4, 0.0), -0.5, 0.5)
    energy = jnp.clip(2.5 + 1.0 * jax.random.uniform(key_list[2], (NODES, ELEMS), jnp.float32) ** shard_levels(key_list[2], (NODES, ELEMS), ((1, 32),), -0.2, 0.2), 2.5, 3.5)
    face_link = draw_face_link(jax.random.fold_in(key_list[8], 71), 0)
    owner_rank_keys = jax.random.split(jax.random.fold_in(key_list[4], 1), POINTS // P_DEV)
    owner_rank_turns = jax.random.permutation(jax.random.fold_in(key_list[4], 3), POINTS // P_DEV)
    owner_rank = jax.vmap(lambda own, number: assign_block(jax.random.fold_in(key_list[4], 2), own, number, P_DEV, N_DOM, 1, CAP, 2))(owner_rank_keys, owner_rank_turns).reshape((POINTS, 1))
    owner_element = with_ends(jax.random.randint(key_list[5], (K_OWN, POINTS), 0, E_DEV), jax.random.fold_in(key_list[5], 1), 0, E_DEV - 1).astype(jnp.int32)
    point_offset = jnp.clip(jax.random.uniform(key_list[6], (3, K_OWN, POINTS), jnp.float32, -1.5, 1.5) * shard_levels(key_list[6], (3, K_OWN, POINTS), ((2, 32),), -0.4, 0.0), -1.5, 1.5)
    point_force = centred(key_list[7], (3, POINTS), 1.0, 4.0, ((1, 32),), jnp.float32)
    return {"density": density, "momentum": momentum, "energy": energy, "face_link": face_link, "owner_rank": owner_rank, "owner_element": owner_element, "point_offset": point_offset, "point_force": point_force}


TIME_STEP = 0.005
SPREAD_WIDTH = 0.5
LIFT_FACTOR = 6.0
HEAT_RATIO = 1.4

def invert_small(matrix):
    order = matrix.shape[0]
    augmented = np.concatenate([np.array(matrix), np.eye(order)], axis=1)
    for column in range(order):
        pivot = column + int(np.argmax(np.abs(augmented[column:, column])))
        saved = augmented[column].copy()
        augmented[column] = augmented[pivot]
        augmented[pivot] = saved
        augmented[column] = augmented[column] / augmented[column, column]
        for other in range(order):
            if other != column:
                augmented[other] = augmented[other] - augmented[other, column] * augmented[column]
    return augmented[:, order:]

def basis_tables():
    gll_nodes = np.array([-1.0, -math.sqrt(0.2), math.sqrt(0.2), 1.0])
    weights = np.array([1.0 / np.prod([gll_nodes[a] - gll_nodes[c] for c in range(4) if c != a]) for a in range(4)])
    nodal_derivative = np.zeros((4, 4))
    for a in range(4):
        for b in range(4):
            if a != b:
                nodal_derivative[a, b] = weights[b] / weights[a] / (gll_nodes[a] - gll_nodes[b])
        nodal_derivative[a, a] = -np.sum(nodal_derivative[a])
    vandermonde = np.stack([np.ones(4), gll_nodes, 1.5 * gll_nodes ** 2 - 0.5, 2.5 * gll_nodes ** 3 - 1.5 * gll_nodes], axis=1)
    damping = np.array([1.0, 1.0, 1.0, 0.75])
    one_dim = vandermonde * damping[None, :] @ invert_small(vandermonde)
    identity = np.eye(4)
    stacked_derivatives = np.concatenate([np.kron(identity, np.kron(identity, nodal_derivative)), np.kron(identity, np.kron(nodal_derivative, identity)), np.kron(nodal_derivative, np.kron(identity, identity))], axis=1)
    modal_filter = np.kron(one_dim, np.kron(one_dim, one_dim))
    node_index = np.arange(64)
    node_coords = np.stack([gll_nodes[node_index % 4], gll_nodes[node_index // 4 % 4], gll_nodes[node_index // 16]])
    return (jnp.asarray(stacked_derivatives, jnp.float32), jnp.asarray(modal_filter, jnp.float32), jnp.asarray(node_coords, jnp.float32))

def face_traces(conserved_fields):
    mesh_elements = conserved_fields.shape[-1]
    lattice = conserved_fields.reshape(5, 4, 4, 4, mesh_elements)
    surfaces = [lattice[:, :, :, 0], lattice[:, :, :, 3], lattice[:, :, 0, :], lattice[:, :, 3, :], lattice[:, 0], lattice[:, 3]]
    return jnp.stack([surface.reshape(5, 16, mesh_elements) for surface in surfaces], axis=2).reshape(80, 6 * mesh_elements)

def lift_faces(correction, mesh_elements):
    lattice = jnp.zeros((5, 4, 4, 4, mesh_elements), jnp.float32)
    lattice = lattice.at[:, :, :, 0].add(correction[:, :, 0].reshape(5, 4, 4, mesh_elements))
    lattice = lattice.at[:, :, :, 3].add(correction[:, :, 1].reshape(5, 4, 4, mesh_elements))
    lattice = lattice.at[:, :, 0, :].add(correction[:, :, 2].reshape(5, 4, 4, mesh_elements))
    lattice = lattice.at[:, :, 3, :].add(correction[:, :, 3].reshape(5, 4, 4, mesh_elements))
    lattice = lattice.at[:, 0].add(correction[:, :, 4].reshape(5, 4, 4, mesh_elements))
    lattice = lattice.at[:, 3].add(correction[:, :, 5].reshape(5, 4, 4, mesh_elements))
    return lattice.reshape(5, 64, mesh_elements)

def primitive(conserved_fields):
    velocity = conserved_fields[1:4] / conserved_fields[0]
    pressure = (HEAT_RATIO - 1.0) * (conserved_fields[4] - 0.5 * lax.optimization_barrier(jnp.sum(conserved_fields[1:4] * velocity, axis=0)))
    return (velocity, pressure)

def flux_along(conserved_fields, velocity, pressure, direction):
    along = velocity[direction]
    result = [conserved_fields[1 + direction], conserved_fields[1] * along, conserved_fields[2] * along, conserved_fields[3] * along, (conserved_fields[4] + pressure) * along]
    result[1 + direction] = result[1 + direction] + pressure
    return jnp.stack(result)

def device_rate(conserved_fields, own_traces, neighbours, source, tables):
    stacked_derivatives = tables[0]
    mesh_elements = conserved_fields.shape[-1]
    velocity, pressure = primitive(conserved_fields)
    numerical_fluxes = jnp.stack([flux_along(conserved_fields, velocity, pressure, d) for d in range(3)], axis=1)
    volume_term = jnp.einsum('ki,rit->rkt', stacked_derivatives, numerical_fluxes.reshape(5, 192, mesh_elements), precision=lax.Precision.HIGHEST)
    inner = own_traces.reshape(5, 16, 6, mesh_elements)
    outer = neighbours.reshape(5, 16, 6, mesh_elements)
    inner_velocity, inner_pressure = primitive(inner)
    outer_velocity, outer_pressure = primitive(outer)
    inner_sound = jnp.sqrt(HEAT_RATIO * inner_pressure / inner[0])
    outer_sound = jnp.sqrt(HEAT_RATIO * outer_pressure / outer[0])
    pieces = []
    for s in range(6):
        d = s // 2
        outward = 1.0 if s % 2 else -1.0
        inside = inner[:, :, s]
        outside = outer[:, :, s]
        inside_flux = flux_along(inside, inner_velocity[:, :, s], inner_pressure[:, s], d)
        outside_flux = flux_along(outside, outer_velocity[:, :, s], outer_pressure[:, s], d)
        wave_speed = jnp.maximum(jnp.abs(inner_velocity[d, :, s]) + inner_sound[:, s], jnp.abs(outer_velocity[d, :, s]) + outer_sound[:, s])
        numerical = 0.5 * outward * (inside_flux + outside_flux) - 0.5 * wave_speed * (outside - inside)
        pieces.append(LIFT_FACTOR * (numerical - outward * inside_flux))
    correction = jnp.stack(pieces, axis=2)
    tendency = -volume_term - lift_faces(correction, mesh_elements)
    momentum_rows = tendency[1:4] + source
    energy_row = tendency[4] + lax.optimization_barrier(jnp.sum(source * velocity, axis=0))
    return jnp.concatenate([tendency[:1], momentum_rows, energy_row[None]], axis=0)

def smooth(conserved_fields, modal_filter):
    return jnp.einsum('ki,rit->rkt', modal_filter, conserved_fields, precision=lax.Precision.HIGHEST)

def spread_points(forces, offsets, node_coords):
    distance = lax.optimization_barrier(jnp.sum((node_coords[:, :, None] - offsets[:, None, :]) ** 2, axis=0))
    return forces[:, None, :] * jnp.exp(-distance / SPREAD_WIDTH)[None]

def invert_link(links, faces, pool_size):
    filled = jnp.zeros((pool_size,), jnp.int32).at[links].set(jnp.arange(faces, dtype=jnp.int32))
    return filled[faces:]

def to_groups(array):
    count = array.shape[0]
    return array.reshape(count, NODES, N_GROUP, N_DOM, E_DEV).transpose(2, 3, 0, 1, 4)

def from_groups(array):
    count = array.shape[2]
    return array.transpose(2, 3, 0, 1, 4).reshape(count, NODES, ELEMS)

def take_columns(table, columns):
    return table[:, columns]

def reference(density, momentum, energy, face_link, owner_rank, owner_element, point_offset, point_force):
    tables = basis_tables()
    faces = 6 * E_DEV
    shared = N_DOM * SF
    pool_size = faces + shared + 2 * GF
    start_fields = jnp.concatenate([density[None], momentum, energy[None]], axis=0)
    point_index = jnp.arange(POINTS, dtype=jnp.int32)
    group_index = point_index // (P_DEV * N_DOM)
    targets = group_index[None, :] * (N_DOM * E_DEV) + owner_rank[:, 0][None, :] * E_DEV + owner_element
    contrib = spread_points(jnp.tile(point_force, (1, K_OWN)), point_offset.reshape(3, K_OWN * POINTS), tables[2])
    source = jnp.zeros((3, NODES, ELEMS), jnp.float32).at[:, :, targets.reshape(K_OWN * POINTS)].add(contrib)
    source_groups = to_groups(source)

    def inverse_rows(links):
        return jax.vmap(lambda row: invert_link(row, faces, pool_size))(links)

    def global_rate(conserved_fields):
        groups = to_groups(conserved_fields)

        def send_rims(item):
            block, links = item
            traces = jax.vmap(face_traces)(block)
            inverse = inverse_rows(links)
            return jax.vmap(take_columns)(traces, inverse[:, shared:])
        rims = lax.map(send_rims, (groups, face_link))
        below = jnp.roll(rims, 1, axis=0)[..., GF:]
        above = jnp.roll(rims, -1, axis=0)[..., :GF]

        def group_update_rate(item):
            block, links, lower, upper, forcing = item
            traces = jax.vmap(face_traces)(block)
            inverse = inverse_rows(links)
            outgoing = jax.vmap(take_columns)(traces, inverse[:, :shared]).reshape(N_DOM, 80, N_DOM, SF)
            incoming = outgoing.transpose(2, 1, 0, 3).reshape(N_DOM, 80, shared)
            trace_pool = jnp.concatenate([traces, incoming, lower, upper], axis=2)
            neighbours = jax.vmap(take_columns)(trace_pool, links)
            return jax.vmap(lambda a, b, c, e: device_rate(a, b, c, e, tables))(block, traces, neighbours, forcing)
        rates = lax.map(group_update_rate, (groups, face_link, below, above, source_groups))
        return from_groups(rates)
    rate_start = global_rate(start_fields)
    section_fields = smooth(start_fields + TIME_STEP * rate_start, tables[1])
    tendency = global_rate(section_fields)
    final_fields = smooth(0.75 * start_fields + 0.25 * (section_fields + TIME_STEP * tendency), tables[1])
    return (final_fields[0], final_fields[1:4], final_fields[4], tendency)
```

```python
import functools
import math

import jax
import jax.numpy as jnp
import numpy as np
from jax import lax
from jax.experimental import pallas as pl
from jax.experimental.pallas import tpu as pltpu
from jax.sharding import PartitionSpec as P

CAP = 32
TIME_STEP = 0.005
SPREAD_WIDTH = 0.5
LIFT_FACTOR = 6.0
HEAT_RATIO = 1.4
LANES = 128
NODES = 64
ROWS = 80
MESH = pl.DeviceIdType.MESH
F32 = jnp.float32
BF16 = jnp.bfloat16


def basis_tables():
    nodes = np.array([-1.0, -math.sqrt(0.2), math.sqrt(0.2), 1.0])
    weights = np.array(
        [1.0 / np.prod([nodes[a] - nodes[c] for c in range(4) if c != a]) for a in range(4)]
    )
    deriv = np.zeros((4, 4))
    for a in range(4):
        for b in range(4):
            if a != b:
                deriv[a, b] = weights[b] / weights[a] / (nodes[a] - nodes[b])
        deriv[a, a] = -np.sum(deriv[a])
    vander = np.stack(
        [np.ones(4), nodes, 1.5 * nodes**2 - 0.5, 2.5 * nodes**3 - 1.5 * nodes], axis=1
    )
    one_dim = vander * np.array([1.0, 1.0, 1.0, 0.75])[None, :] @ np.linalg.inv(vander)
    eye = np.eye(4)
    dcat = np.concatenate(
        [
            np.kron(eye, np.kron(eye, deriv)),
            np.kron(eye, np.kron(deriv, eye)),
            np.kron(deriv, np.kron(eye, eye)),
        ],
        axis=1,
    )
    filt = np.kron(one_dim, np.kron(one_dim, one_dim))
    return nodes, dcat, filt


def split_table(table):
    table = np.asarray(table, np.float32)
    high = table.astype(BF16)
    low = (table - high.astype(np.float32)).astype(BF16)
    top = np.concatenate([high, high], axis=1)
    bottom = np.concatenate([low, np.zeros_like(low)], axis=1)
    return np.concatenate([top, bottom], axis=0)


def split2(x):
    high = x.astype(BF16)
    return high, (x - high.astype(F32)).astype(BF16)


def split3(x):
    high = x.astype(BF16)
    rest = x - high.astype(F32)
    middle = rest.astype(BF16)
    return high, middle, (rest - middle.astype(F32)).astype(BF16)


def dot_nt(a, b):
    return lax.dot_general(a, b, (((1,), (1,)), ((), ())), preferred_element_type=F32)


def pick_lanes(x, index):
    return jnp.take_along_axis(x, index, axis=1, mode="promise_in_bounds")


def state_of(rows):
    inverse = 1.0 / rows[0]
    vel = [rows[1 + c] * inverse for c in range(3)]
    press = (HEAT_RATIO - 1.0) * (
        rows[4] - 0.5 * (rows[1] * vel[0] + rows[2] * vel[1] + rows[3] * vel[2])
    )
    return inverse, vel, press


def flux_of(rows, vel, press, d):
    along = vel[d]
    out = [
        rows[1 + d],
        rows[1] * along,
        rows[2] * along,
        rows[3] * along,
        (rows[4] + press) * along,
    ]
    out[1 + d] = out[1 + d] + press
    return out


def kernel(
    nd, ng, nodes,
    den, mom, ene, link, rank, elem, off, force, dmat, fmat,
    o_den, o_mom, o_ene, o_tend,
    q, q1, td, tr, nb, t3, oh, lk, fx, xf, ex, src, ohe, ct,
    s1, r1, s2, r2, rs, rr, send_sem, recv_sem, rim_send_sem, rim_recv_sem,
):
    width = den.shape[1]
    cols = width // LANES
    blocks = 6 * cols
    shared = nd * (width // 32)
    shared_blocks = shared // LANES
    extra = shared_blocks + 2
    me = lax.axis_index("dom")
    group = lax.axis_index("group")
    up, down = lax.rem(group + 1, ng), lax.rem(group + ng - 1, ng)

    barrier = pltpu.get_barrier_semaphore()
    for d in range(1, nd):
        pl.semaphore_signal(
            barrier, inc=1, device_id={"dom": lax.rem(me + d, nd)}, device_id_type=MESH
        )
    for target in (up, down):
        pl.semaphore_signal(barrier, inc=1, device_id={"group": target}, device_id_type=MESH)

    def at(v, c):
        return (v * cols + c) * NODES

    for c in range(cols):
        lanes = slice(c * LANES, (c + 1) * LANES)
        q[at(0, c) : at(0, c) + NODES, :] = den[:, lanes]
        for v in range(3):
            q[at(1 + v, c) : at(1 + v, c) + NODES, :] = mom[v, :, lanes]
        q[at(4, c) : at(4, c) + NODES, :] = ene[:, lanes]

    row_ids = lax.broadcasted_iota(jnp.int32, (extra * LANES, LANES), 0) + 6 * width
    for b in range(blocks):
        part = link[0:1, b * LANES : (b + 1) * LANES]
        lk[b] = jnp.broadcast_to(part, (8, LANES))
        oh[:, b * LANES : (b + 1) * LANES] = jnp.where(row_ids == part, 1.0, 0.0).astype(BF16)

    def fill_traces(ref):
        for c in range(cols):
            for v in range(5):
                base = at(v, c)
                for t in range(6):
                    dst = (t * cols + c) * ROWS + v * 16
                    if t < 2:
                        tr[dst : dst + 16, :] = ref[pl.ds(base + 3 * t, 16, 4), :]
                    elif t < 4:
                        for k in range(4):
                            first = base + 16 * k + 12 * (t - 2)
                            tr[dst + 4 * k : dst + 4 * k + 4, :] = ref[first : first + 4, :]
                    else:
                        first = base + 48 * (t - 4)
                        tr[dst : dst + 16, :] = ref[first : first + 16, :]

    def prepare(send, section):
        for b in range(blocks):
            parts = split3(tr[b * ROWS : (b + 1) * ROWS, :])
            for s in range(3):
                t3[s * ROWS : (s + 1) * ROWS, b * LANES : (b + 1) * LANES] = parts[s]
        out = dot_nt(t3[...], oh[...])
        out = out[:ROWS] + out[ROWS : 2 * ROWS] + out[2 * ROWS :]
        for j in range(shared_blocks):
            block = jnp.concatenate(
                [out[:, j * LANES : (j + 1) * LANES], jnp.zeros((LANES - ROWS, LANES), F32)], axis=0
            )
            flipped = block.T
            for p in range(8):
                send[j * 8 + p, 0:16, :] = flipped[p * 16 : (p + 1) * 16, :]
        for side in range(2):
            first = (shared_blocks + side) * LANES
            rs[section, side] = out[:, first : first + LANES]

    def copies(send, receive, section):
        made = []
        for d in range(1, nd):
            peer = lax.rem(me + d, nd)
            made.append(
                pltpu.make_async_remote_copy(
                    src_ref=send.at[peer],
                    dst_ref=receive.at[me],
                    send_sem=send_sem.at[section, d],
                    recv_sem=recv_sem.at[section, d],
                    device_id={"dom": peer},
                    device_id_type=MESH,
                )
            )
        for side, target in ((0, down), (1, up)):
            made.append(
                pltpu.make_async_remote_copy(
                    src_ref=rs.at[section, side],
                    dst_ref=rr.at[section, 1 - side],
                    send_sem=rim_send_sem.at[section, side],
                    recv_sem=rim_recv_sem.at[section, 1 - side],
                    device_id={"group": target},
                    device_id_type=MESH,
                )
            )
        return made

    def waits(send, receive, section):
        for d in range(1, nd):
            source = lax.rem(me + nd - d, nd)
            pltpu.make_async_remote_copy(
                src_ref=send.at[lax.rem(me + d, nd)],
                dst_ref=receive.at[source],
                send_sem=send_sem.at[section, d],
                recv_sem=recv_sem.at[section, d],
                device_id={"dom": lax.rem(me + d, nd)},
                device_id_type=MESH,
            ).wait()
        for side, target in ((0, down), (1, up)):
            pltpu.make_async_remote_copy(
                src_ref=rs.at[section, side],
                dst_ref=rr.at[section, side],
                send_sem=rim_send_sem.at[section, side],
                recv_sem=rim_recv_sem.at[section, side],
                device_id={"group": target},
                device_id_type=MESH,
            ).wait()

    def gather_own(ob, carry):
        index = lk[ob]
        lane = index & (LANES - 1)
        where = index >> 7
        acc = [jnp.zeros((8, LANES), F32) for _ in range(10)]
        for sb in range(blocks):
            hit = where == sb
            for r in range(10):
                first = sb * ROWS + r * 8
                acc[r] = jnp.where(hit, pick_lanes(tr[first : first + 8, :], lane), acc[r])
        for r in range(10):
            nb[ob, r * 8 : r * 8 + 8, :] = acc[r]
        return carry

    def gather_arrived(ob, carry):
        index = lk[ob]
        lane = index & (LANES - 1)
        where = index >> 7
        for r in range(10):
            acc = nb[ob, r * 8 : r * 8 + 8, :]
            for sb in range(extra):
                acc = jnp.where(
                    where == blocks + sb, pick_lanes(ex[sb, r * 8 : r * 8 + 8, :], lane), acc
                )
            nb[ob, r * 8 : r * 8 + 8, :] = acc
        return carry

    def unpack(receive, section):
        for j in range(shared_blocks):
            block = jnp.concatenate([receive[j * 8 + p, 0:16, :] for p in range(8)], axis=0)
            ex[j] = block.T[:ROWS]
        for side in range(2):
            ex[shared_blocks + side] = rr[section, side]

    def volume(ref):
        for c in range(cols):
            lanes = slice(c * LANES, (c + 1) * LANES)
            for n in range(0, NODES, 16):
                rows = [ref[at(v, c) + n : at(v, c) + n + 16, :] for v in range(5)]
                _, vel, press = state_of(rows)
                for d in range(3):
                    flux = flux_of(rows, vel, press, d)
                    for v in range(5):
                        high, low = split2(flux[v])
                        fx[v, d * NODES + n : d * NODES + n + 16, lanes] = high
                        fx[v, (3 + d) * NODES + n : (3 + d) * NODES + n + 16, lanes] = low
        for v in range(5):
            out = jnp.dot(dmat[...], fx[v], preferred_element_type=F32)
            out = -(out[:NODES] + out[NODES:])
            for c in range(cols):
                td[at(v, c) : at(v, c) + NODES, :] = out[:, c * LANES : (c + 1) * LANES]

    def surface():
        for t in range(6):
            d = t // 2
            outward = 1.0 if t % 2 else -1.0
            for c in range(cols):
                b = t * cols + c
                inside = [tr[b * ROWS + v * 16 : b * ROWS + v * 16 + 16, :] for v in range(5)]
                outside = [nb[b, v * 16 : v * 16 + 16, :] for v in range(5)]
                inv_a, vel_a, press_a = state_of(inside)
                inv_b, vel_b, press_b = state_of(outside)
                lam = jnp.maximum(
                    jnp.abs(vel_a[d]) + jnp.sqrt(HEAT_RATIO * press_a * inv_a),
                    jnp.abs(vel_b[d]) + jnp.sqrt(HEAT_RATIO * press_b * inv_b),
                )
                lam = (0.5 * LIFT_FACTOR) * lam
                flux_a = flux_of(inside, vel_a, press_a, d)
                flux_b = flux_of(outside, vel_b, press_b, d)
                for v in range(5):
                    fix = lam * (outside[v] - inside[v]) - (0.5 * LIFT_FACTOR * outward) * (
                        flux_b[v] - flux_a[v]
                    )
                    base = at(v, c)
                    if t < 2:
                        place = pl.ds(base + 3 * t, 16, 4)
                        td[place, :] = td[place, :] + fix
                    elif t < 4:
                        for k in range(4):
                            first = base + 16 * k + 12 * (t - 2)
                            td[first : first + 4, :] = (
                                td[first : first + 4, :] + fix[4 * k : 4 * k + 4, :]
                            )
                    else:
                        first = base + 48 * (t - 4)
                        td[first : first + 16, :] = td[first : first + 16, :] + fix

    def finish(ref, second):
        for c in range(cols):
            lanes = slice(c * LANES, (c + 1) * LANES)
            for n in range(0, NODES, 16):
                rows = [ref[at(v, c) + n : at(v, c) + n + 16, :] for v in range(5)]
                rate = [td[at(v, c) + n : at(v, c) + n + 16, :] for v in range(5)]
                push = [src[k * NODES + n : k * NODES + n + 16, lanes] for k in range(3)]
                inverse = 1.0 / rows[0]
                work = (push[0] * rows[1] + push[1] * rows[2] + push[2] * rows[3]) * inverse
                rate = [
                    rate[0], rate[1] + push[0], rate[2] + push[1], rate[3] + push[2], rate[4] + work
                ]
                for v in range(5):
                    moved = rows[v] + TIME_STEP * rate[v]
                    if second:
                        o_tend[v, n : n + 16, lanes] = rate[v]
                        moved = 0.75 * q[at(v, c) + n : at(v, c) + n + 16, :] + 0.25 * moved
                    high, low = split2(moved)
                    xf[v, n : n + 16, lanes] = high
                    xf[v, NODES + n : NODES + n + 16, lanes] = low
        for v in range(5):
            out = jnp.dot(fmat[...], xf[v], preferred_element_type=F32)
            out = out[:NODES] + out[NODES:]
            if not second:
                for c in range(cols):
                    q1[at(v, c) : at(v, c) + NODES, :] = out[:, c * LANES : (c + 1) * LANES]
            elif v == 0:
                o_den[...] = out
            elif v == 4:
                o_ene[...] = out
            else:
                o_mom[v - 1] = out

    def pack_points():
        column = jnp.broadcast_to(rank[...].astype(F32), (LANES, LANES))
        across = column.T
        earlier = lax.broadcasted_iota(jnp.int32, (LANES, LANES), 1) < lax.broadcasted_iota(
            jnp.int32, (LANES, LANES), 0
        )
        place = jnp.sum(
            jnp.where((column == across) & earlier, 1.0, 0.0), axis=1, keepdims=True
        )
        target = column[:, 0:1] * float(LANES) + place
        slots = lax.broadcasted_iota(jnp.int32, (LANES, nd * LANES), 1).astype(F32)
        total = None
        for k in range(4):
            spread = jnp.where(target + float(k * CAP) == slots, 1.0, 0.0).astype(BF16)
            data = jnp.concatenate(
                [elem[k : k + 1, :].astype(F32)]
                + [off[x, k : k + 1, :] for x in range(3)]
                + [force[...], jnp.zeros((1, LANES), F32)],
                axis=0,
            )
            stacked = jnp.concatenate([part.astype(F32) for part in split3(data)], axis=0)
            out = jnp.dot(stacked.astype(BF16), spread, preferred_element_type=F32)
            total = out if total is None else total + out
        total = total[:8] + total[8:16] + total[16:]
        for a in range(nd):
            s1[a, 16:24, :] = total[:, a * LANES : (a + 1) * LANES]

    def spread_sources():
        n = lax.broadcasted_iota(jnp.int32, (NODES, LANES), 0)
        places = [n & 3, (n >> 2) & 3, n >> 4]
        coords = [
            jnp.where(
                p < 2,
                jnp.where(p == 0, float(nodes[0]), float(nodes[1])),
                jnp.where(p == 2, float(nodes[2]), float(nodes[3])),
            )
            for p in places
        ]
        element_ids = lax.broadcasted_iota(jnp.int32, (width, LANES), 0).astype(F32)
        for b in range(nd):
            lanes = slice(b * LANES, (b + 1) * LANES)
            tile = r1[b, 16:24, :]
            ohe[:, lanes] = jnp.where(element_ids == tile[0:1, :], 1.0, 0.0).astype(BF16)
            gap = [coords[x] - tile[1 + x : 2 + x, :] for x in range(3)]
            distance = gap[0] * gap[0] + gap[1] * gap[1] + gap[2] * gap[2]
            weight = jnp.exp(distance * (-1.0 / SPREAD_WIDTH))
            for x in range(3):
                high, low = split2(weight * tile[4 + x : 5 + x, :])
                ct[x * NODES : (x + 1) * NODES, lanes] = high
                ct[(3 + x) * NODES : (4 + x) * NODES, lanes] = low
        out = dot_nt(ct[...], ohe[...])
        src[...] = out[: 3 * NODES] + out[3 * NODES :]

    fill_traces(q)
    pack_points()
    prepare(s1, 0)
    pl.semaphore_wait(barrier, nd + 1)
    for copy in copies(s1, r1, 0):
        copy.start()
    r1[me] = s1[me]
    volume(q)
    lax.fori_loop(0, blocks, gather_own, 0)
    waits(s1, r1, 0)
    unpack(r1, 0)
    spread_sources()
    lax.fori_loop(0, blocks, gather_arrived, 0)
    surface()
    finish(q, False)

    fill_traces(q1)
    prepare(s2, 1)
    for copy in copies(s2, r2, 1):
        copy.start()
    r2[me] = s2[me]
    volume(q1)
    lax.fori_loop(0, blocks, gather_own, 0)
    waits(s2, r2, 1)
    unpack(r2, 1)
    lax.fori_loop(0, blocks, gather_arrived, 0)
    surface()
    finish(q1, True)


def body(density, momentum, energy, face_link, owner_rank, owner_element, offsets, forces):
    nd, ng = lax.axis_size("dom"), lax.axis_size("group")
    width = density.shape[1]
    cols = width // LANES
    blocks = 6 * cols
    extra = nd * (width // 32) // LANES + 2
    nodes, dcat, filt = basis_tables()
    vmem = pl.BlockSpec(memory_space=pltpu.VMEM)
    shape = jax.ShapeDtypeStruct
    return pl.pallas_call(
        functools.partial(kernel, nd, ng, nodes),
        out_shape=(
            shape((NODES, width), F32),
            shape((3, NODES, width), F32),
            shape((NODES, width), F32),
            shape((5, NODES, width), F32),
        ),
        in_specs=[vmem] * 10,
        out_specs=(vmem,) * 4,
        scratch_shapes=[
            pltpu.VMEM((5 * cols * NODES, LANES), F32),
            pltpu.VMEM((5 * cols * NODES, LANES), F32),
            pltpu.VMEM((5 * cols * NODES, LANES), F32),
            pltpu.VMEM((blocks * ROWS, LANES), F32),
            pltpu.VMEM((blocks, ROWS, LANES), F32),
            pltpu.VMEM((3 * ROWS, blocks * LANES), BF16),
            pltpu.VMEM((extra * LANES, blocks * LANES), BF16),
            pltpu.VMEM((blocks, 8, LANES), jnp.int32),
            pltpu.VMEM((5, 6 * NODES, width), BF16),
            pltpu.VMEM((5, 2 * NODES, width), BF16),
            pltpu.VMEM((extra, ROWS, LANES), F32),
            pltpu.VMEM((3 * NODES, width), F32),
            pltpu.VMEM((width, nd * LANES), BF16),
            pltpu.VMEM((6 * NODES, nd * LANES), BF16),
            pltpu.VMEM((nd, 24, LANES), F32),
            pltpu.VMEM((nd, 24, LANES), F32),
            pltpu.VMEM((nd, 16, LANES), F32),
            pltpu.VMEM((nd, 16, LANES), F32),
            pltpu.VMEM((2, 2, ROWS, LANES), F32),
            pltpu.VMEM((2, 2, ROWS, LANES), F32),
            pltpu.SemaphoreType.DMA((2, nd)),
            pltpu.SemaphoreType.DMA((2, nd)),
            pltpu.SemaphoreType.DMA((2, 2)),
            pltpu.SemaphoreType.DMA((2, 2)),
        ],
        compiler_params=pltpu.CompilerParams(
            collective_id=0, has_side_effects=True, vmem_limit_bytes=48 * 1024 * 1024
        ),
    )(
        density,
        momentum,
        energy,
        face_link.reshape(1, 6 * width),
        owner_rank,
        owner_element,
        offsets,
        forces,
        jnp.asarray(split_table(dcat)),
        jnp.asarray(split_table(filt)),
    )


def solution(mesh):
    element = P(None, ("group", "dom"))
    stacked = P(None, None, ("group", "dom"))
    return jax.shard_map(
        body,
        mesh=mesh,
        in_specs=(
            element,
            stacked,
            element,
            P("group", "dom", None),
            P(("group", "dom"), None),
            element,
            stacked,
            element,
        ),
        out_specs=(element, stacked, element, stacked),
        check_vma=False,
    )
```

```python
import functools
import math

import jax
import jax.numpy as jnp
import numpy as np
from jax import lax
from jax.experimental import pallas as pl
from jax.experimental.pallas import tpu as pltpu
from jax.sharding import PartitionSpec as P

CAP = 32
TIME_STEP = 0.005
SPREAD_WIDTH = 0.5
LIFT_FACTOR = 6.0
HEAT_RATIO = 1.4
LANES = 128
NODES = 64
ROWS = 80
MESH = pl.DeviceIdType.MESH
F32 = jnp.float32
BF16 = jnp.bfloat16


def basis_tables():
    nodes = np.array([-1.0, -math.sqrt(0.2), math.sqrt(0.2), 1.0])
    weights = np.array(
        [1.0 / np.prod([nodes[a] - nodes[c] for c in range(4) if c != a]) for a in range(4)]
    )
    deriv = np.zeros((4, 4))
    for a in range(4):
        for b in range(4):
            if a != b:
                deriv[a, b] = weights[b] / weights[a] / (nodes[a] - nodes[b])
        deriv[a, a] = -np.sum(deriv[a])
    vander = np.stack(
        [np.ones(4), nodes, 1.5 * nodes**2 - 0.5, 2.5 * nodes**3 - 1.5 * nodes], axis=1
    )
    one_dim = vander * np.array([1.0, 1.0, 1.0, 0.75])[None, :] @ np.linalg.inv(vander)
    eye = np.eye(4)
    dcat = np.concatenate(
        [
            np.kron(eye, np.kron(eye, deriv)),
            np.kron(eye, np.kron(deriv, eye)),
            np.kron(deriv, np.kron(eye, eye)),
        ],
        axis=1,
    )
    filt = np.kron(one_dim, np.kron(one_dim, one_dim))
    return nodes, dcat, filt


def split_table(table):
    table = np.asarray(table, np.float32)
    high = table.astype(BF16)
    low = (table - high.astype(np.float32)).astype(BF16)
    top = np.concatenate([high, high], axis=1)
    bottom = np.concatenate([low, np.zeros_like(low)], axis=1)
    return np.concatenate([top, bottom], axis=0)


def split2(x):
    high = x.astype(BF16)
    return high, (x - high.astype(F32)).astype(BF16)


def split3(x):
    high = x.astype(BF16)
    rest = x - high.astype(F32)
    middle = rest.astype(BF16)
    return high, middle, (rest - middle.astype(F32)).astype(BF16)


def dot_nt(a, b):
    return lax.dot_general(a, b, (((1,), (1,)), ((), ())), preferred_element_type=F32)


def pick_lanes(x, index):
    return jnp.take_along_axis(x, index, axis=1, mode="promise_in_bounds")


def state_of(rows):
    inverse = 1.0 / rows[0]
    vel = [rows[1 + c] * inverse for c in range(3)]
    press = (HEAT_RATIO - 1.0) * (
        rows[4] - 0.5 * (rows[1] * vel[0] + rows[2] * vel[1] + rows[3] * vel[2])
    )
    return inverse, vel, press


def flux_of(rows, vel, press, d):
    along = vel[d]
    out = [
        rows[1 + d],
        rows[1] * along,
        rows[2] * along,
        rows[3] * along,
        (rows[4] + press) * along,
    ]
    out[1 + d] = out[1 + d] + press
    return out


def kernel(
    nd, ng, nodes,
    den, mom, ene, link, rank, elem, off, force, dmat, fmat,
    o_den, o_mom, o_ene, o_tend,
    q, q1, td, tr, nb, t3, oh, tall, got, index, index_sem, fx, xf, ex, src, ohe, ct,
    s1, r1, s2, r2, rs, rr, send_sem, recv_sem, rim_send_sem, rim_recv_sem,
):
    width = den.shape[1]
    cols = width // LANES
    blocks = 6 * cols
    shared = nd * (width // 32)
    shared_blocks = shared // LANES
    extra = shared_blocks + 2
    me = lax.axis_index("dom")
    group = lax.axis_index("group")
    up, down = lax.rem(group + 1, ng), lax.rem(group + ng - 1, ng)

    fetch = pltpu.make_async_copy(link, index, index_sem)
    fetch.start()
    barrier = pltpu.get_barrier_semaphore()
    for d in range(1, nd):
        pl.semaphore_signal(
            barrier, inc=1, device_id={"dom": lax.rem(me + d, nd)}, device_id_type=MESH
        )
    for target in (up, down):
        pl.semaphore_signal(barrier, inc=1, device_id={"group": target}, device_id_type=MESH)

    def at(v, c):
        return (v * cols + c) * NODES

    for c in range(cols):
        lanes = slice(c * LANES, (c + 1) * LANES)
        q[at(0, c) : at(0, c) + NODES, :] = den[:, lanes]
        for v in range(3):
            q[at(1 + v, c) : at(1 + v, c) + NODES, :] = mom[v, :, lanes]
        q[at(4, c) : at(4, c) + NODES, :] = ene[:, lanes]

    row_ids = lax.broadcasted_iota(jnp.int32, (extra * LANES, LANES), 0) + 6 * width
    for b in range(blocks):
        part = link[0:1, b * LANES : (b + 1) * LANES]
        oh[:, b * LANES : (b + 1) * LANES] = jnp.where(row_ids == part, 1.0, 0.0).astype(BF16)

    def fill_traces(ref):
        for c in range(cols):
            for v in range(5):
                base = at(v, c)
                for t in range(6):
                    dst = (t * cols + c) * ROWS + v * 16
                    if t < 2:
                        tr[dst : dst + 16, :] = ref[pl.ds(base + 3 * t, 16, 4), :]
                    elif t < 4:
                        for k in range(4):
                            first = base + 16 * k + 12 * (t - 2)
                            tr[dst + 4 * k : dst + 4 * k + 4, :] = ref[first : first + 4, :]
                    else:
                        first = base + 48 * (t - 4)
                        tr[dst : dst + 16, :] = ref[first : first + 16, :]

    def prepare(send, section):
        for b in range(blocks):
            parts = split3(tr[b * ROWS : (b + 1) * ROWS, :])
            for s in range(3):
                t3[s * ROWS : (s + 1) * ROWS, b * LANES : (b + 1) * LANES] = parts[s]
        out = dot_nt(t3[...], oh[...])
        out = out[:ROWS] + out[ROWS : 2 * ROWS] + out[2 * ROWS :]
        for j in range(shared_blocks):
            block = jnp.concatenate(
                [out[:, j * LANES : (j + 1) * LANES], jnp.zeros((LANES - ROWS, LANES), F32)], axis=0
            )
            flipped = block.T
            for p in range(8):
                send[j * 8 + p, 0:16, :] = flipped[p * 16 : (p + 1) * 16, :]
        for side in range(2):
            first = (shared_blocks + side) * LANES
            rs[section, side] = out[:, first : first + LANES]

    def copies(send, receive, section):
        made = []
        for d in range(1, nd):
            peer = lax.rem(me + d, nd)
            made.append(
                pltpu.make_async_remote_copy(
                    src_ref=send.at[peer],
                    dst_ref=receive.at[me],
                    send_sem=send_sem.at[section, d],
                    recv_sem=recv_sem.at[section, d],
                    device_id={"dom": peer},
                    device_id_type=MESH,
                )
            )
        for side, target in ((0, down), (1, up)):
            made.append(
                pltpu.make_async_remote_copy(
                    src_ref=rs.at[section, side],
                    dst_ref=rr.at[section, 1 - side],
                    send_sem=rim_send_sem.at[section, side],
                    recv_sem=rim_recv_sem.at[section, 1 - side],
                    device_id={"group": target},
                    device_id_type=MESH,
                )
            )
        return made

    def waits(send, receive, section):
        for d in range(1, nd):
            source = lax.rem(me + nd - d, nd)
            pltpu.make_async_remote_copy(
                src_ref=send.at[lax.rem(me + d, nd)],
                dst_ref=receive.at[source],
                send_sem=send_sem.at[section, d],
                recv_sem=recv_sem.at[section, d],
                device_id={"dom": lax.rem(me + d, nd)},
                device_id_type=MESH,
            ).wait()
        for side, target in ((0, down), (1, up)):
            pltpu.make_async_remote_copy(
                src_ref=rs.at[section, side],
                dst_ref=rr.at[section, side],
                send_sem=rim_send_sem.at[section, side],
                recv_sem=rim_recv_sem.at[section, side],
                device_id={"group": target},
                device_id_type=MESH,
            ).wait()

    def turn_traces():
        for b in range(blocks):
            block = jnp.concatenate(
                [tr[b * ROWS : (b + 1) * ROWS, :], jnp.zeros((LANES - ROWS, LANES), F32)], axis=0
            )
            tall[b * LANES : (b + 1) * LANES, :] = block.T

    def gather_own():
        def rows_of(ob, carry):
            for r in range(LANES):
                face = ob * LANES + r
                got[pl.ds(face, 1), :] = tall[pl.ds(index[0, face], 1), :]
            return carry

        lax.fori_loop(0, blocks, rows_of, 0)
        for b in range(blocks):
            nb[b] = got[b * LANES : (b + 1) * LANES, :].T[:ROWS]

    def unpack(receive, section):
        for j in range(shared_blocks):
            block = jnp.concatenate([receive[j * 8 + p, 0:16, :] for p in range(8)], axis=0)
            ex[:, j * LANES : (j + 1) * LANES] = block.T[:ROWS]
        for side in range(2):
            first = (shared_blocks + side) * LANES
            ex[:, first : first + LANES] = rr[section, side]

    def gather_arrived():
        parts = split2(ex[...])
        stacked = jnp.concatenate(parts, axis=0)
        out = jnp.dot(stacked, oh[...], preferred_element_type=F32)
        for b in range(blocks):
            lanes = slice(b * LANES, (b + 1) * LANES)
            nb[b] = nb[b] + (out[:ROWS, lanes] + out[ROWS:, lanes])

    def volume(ref):
        for c in range(cols):
            lanes = slice(c * LANES, (c + 1) * LANES)
            for n in range(0, NODES, 16):
                rows = [ref[at(v, c) + n : at(v, c) + n + 16, :] for v in range(5)]
                _, vel, press = state_of(rows)
                for d in range(3):
                    flux = flux_of(rows, vel, press, d)
                    for v in range(5):
                        high, low = split2(flux[v])
                        fx[v, d * NODES + n : d * NODES + n + 16, lanes] = high
                        fx[v, (3 + d) * NODES + n : (3 + d) * NODES + n + 16, lanes] = low
        for v in range(5):
            out = jnp.dot(dmat[...], fx[v], preferred_element_type=F32)
            out = -(out[:NODES] + out[NODES:])
            for c in range(cols):
                td[at(v, c) : at(v, c) + NODES, :] = out[:, c * LANES : (c + 1) * LANES]

    def surface():
        for t in range(6):
            d = t // 2
            outward = 1.0 if t % 2 else -1.0
            for c in range(cols):
                b = t * cols + c
                inside = [tr[b * ROWS + v * 16 : b * ROWS + v * 16 + 16, :] for v in range(5)]
                outside = [nb[b, v * 16 : v * 16 + 16, :] for v in range(5)]
                inv_a, vel_a, press_a = state_of(inside)
                inv_b, vel_b, press_b = state_of(outside)
                lam = jnp.maximum(
                    jnp.abs(vel_a[d]) + jnp.sqrt(HEAT_RATIO * press_a * inv_a),
                    jnp.abs(vel_b[d]) + jnp.sqrt(HEAT_RATIO * press_b * inv_b),
                )
                lam = (0.5 * LIFT_FACTOR) * lam
                flux_a = flux_of(inside, vel_a, press_a, d)
                flux_b = flux_of(outside, vel_b, press_b, d)
                for v in range(5):
                    fix = lam * (outside[v] - inside[v]) - (0.5 * LIFT_FACTOR * outward) * (
                        flux_b[v] - flux_a[v]
                    )
                    base = at(v, c)
                    if t < 2:
                        place = pl.ds(base + 3 * t, 16, 4)
                        td[place, :] = td[place, :] + fix
                    elif t < 4:
                        for k in range(4):
                            first = base + 16 * k + 12 * (t - 2)
                            td[first : first + 4, :] = (
                                td[first : first + 4, :] + fix[4 * k : 4 * k + 4, :]
                            )
                    else:
                        first = base + 48 * (t - 4)
                        td[first : first + 16, :] = td[first : first + 16, :] + fix

    def finish(ref, second):
        for c in range(cols):
            lanes = slice(c * LANES, (c + 1) * LANES)
            for n in range(0, NODES, 16):
                rows = [ref[at(v, c) + n : at(v, c) + n + 16, :] for v in range(5)]
                rate = [td[at(v, c) + n : at(v, c) + n + 16, :] for v in range(5)]
                push = [src[k * NODES + n : k * NODES + n + 16, lanes] for k in range(3)]
                inverse = 1.0 / rows[0]
                work = (push[0] * rows[1] + push[1] * rows[2] + push[2] * rows[3]) * inverse
                rate = [
                    rate[0], rate[1] + push[0], rate[2] + push[1], rate[3] + push[2], rate[4] + work
                ]
                for v in range(5):
                    moved = rows[v] + TIME_STEP * rate[v]
                    if second:
                        o_tend[v, n : n + 16, lanes] = rate[v]
                        moved = 0.75 * q[at(v, c) + n : at(v, c) + n + 16, :] + 0.25 * moved
                    high, low = split2(moved)
                    xf[v, n : n + 16, lanes] = high
                    xf[v, NODES + n : NODES + n + 16, lanes] = low
        for v in range(5):
            out = jnp.dot(fmat[...], xf[v], preferred_element_type=F32)
            out = out[:NODES] + out[NODES:]
            if not second:
                for c in range(cols):
                    q1[at(v, c) : at(v, c) + NODES, :] = out[:, c * LANES : (c + 1) * LANES]
            elif v == 0:
                o_den[...] = out
            elif v == 4:
                o_ene[...] = out
            else:
                o_mom[v - 1] = out

    def pack_points():
        column = jnp.broadcast_to(rank[...].astype(F32), (LANES, LANES))
        across = column.T
        earlier = lax.broadcasted_iota(jnp.int32, (LANES, LANES), 1) < lax.broadcasted_iota(
            jnp.int32, (LANES, LANES), 0
        )
        place = jnp.sum(
            jnp.where((column == across) & earlier, 1.0, 0.0), axis=1, keepdims=True
        )
        target = column[:, 0:1] * float(LANES) + place
        slots = lax.broadcasted_iota(jnp.int32, (LANES, nd * LANES), 1).astype(F32)
        total = None
        for k in range(4):
            spread = jnp.where(target + float(k * CAP) == slots, 1.0, 0.0).astype(BF16)
            data = jnp.concatenate(
                [elem[k : k + 1, :].astype(F32)]
                + [off[x, k : k + 1, :] for x in range(3)]
                + [force[...], jnp.zeros((1, LANES), F32)],
                axis=0,
            )
            stacked = jnp.concatenate([part.astype(F32) for part in split3(data)], axis=0)
            out = jnp.dot(stacked.astype(BF16), spread, preferred_element_type=F32)
            total = out if total is None else total + out
        total = total[:8] + total[8:16] + total[16:]
        for a in range(nd):
            s1[a, 16:24, :] = total[:, a * LANES : (a + 1) * LANES]

    def spread_sources():
        n = lax.broadcasted_iota(jnp.int32, (NODES, LANES), 0)
        places = [n & 3, (n >> 2) & 3, n >> 4]
        coords = [
            jnp.where(
                p < 2,
                jnp.where(p == 0, float(nodes[0]), float(nodes[1])),
                jnp.where(p == 2, float(nodes[2]), float(nodes[3])),
            )
            for p in places
        ]
        element_ids = lax.broadcasted_iota(jnp.int32, (width, LANES), 0).astype(F32)
        for b in range(nd):
            lanes = slice(b * LANES, (b + 1) * LANES)
            tile = r1[b, 16:24, :]
            ohe[:, lanes] = jnp.where(element_ids == tile[0:1, :], 1.0, 0.0).astype(BF16)
            gap = [coords[x] - tile[1 + x : 2 + x, :] for x in range(3)]
            distance = gap[0] * gap[0] + gap[1] * gap[1] + gap[2] * gap[2]
            weight = jnp.exp(distance * (-1.0 / SPREAD_WIDTH))
            for x in range(3):
                high, low = split2(weight * tile[4 + x : 5 + x, :])
                ct[x * NODES : (x + 1) * NODES, lanes] = high
                ct[(3 + x) * NODES : (4 + x) * NODES, lanes] = low
        out = dot_nt(ct[...], ohe[...])
        src[...] = out[: 3 * NODES] + out[3 * NODES :]

    tall[6 * width :, :] = jnp.zeros((extra * LANES, LANES), F32)
    fetch.wait()
    fill_traces(q)
    pack_points()
    prepare(s1, 0)
    pl.semaphore_wait(barrier, nd + 1)
    for copy in copies(s1, r1, 0):
        copy.start()
    r1[me] = s1[me]
    turn_traces()
    volume(q)
    gather_own()
    waits(s1, r1, 0)
    unpack(r1, 0)
    spread_sources()
    gather_arrived()
    surface()
    finish(q, False)

    fill_traces(q1)
    prepare(s2, 1)
    for copy in copies(s2, r2, 1):
        copy.start()
    r2[me] = s2[me]
    turn_traces()
    volume(q1)
    gather_own()
    waits(s2, r2, 1)
    unpack(r2, 1)
    gather_arrived()
    surface()
    finish(q1, True)


def body(density, momentum, energy, face_link, owner_rank, owner_element, offsets, forces):
    nd, ng = lax.axis_size("dom"), lax.axis_size("group")
    width = density.shape[1]
    cols = width // LANES
    blocks = 6 * cols
    extra = nd * (width // 32) // LANES + 2
    nodes, dcat, filt = basis_tables()
    vmem = pl.BlockSpec(memory_space=pltpu.VMEM)
    shape = jax.ShapeDtypeStruct
    return pl.pallas_call(
        functools.partial(kernel, nd, ng, nodes),
        out_shape=(
            shape((NODES, width), F32),
            shape((3, NODES, width), F32),
            shape((NODES, width), F32),
            shape((5, NODES, width), F32),
        ),
        in_specs=[vmem] * 10,
        out_specs=(vmem,) * 4,
        scratch_shapes=[
            pltpu.VMEM((5 * cols * NODES, LANES), F32),
            pltpu.VMEM((5 * cols * NODES, LANES), F32),
            pltpu.VMEM((5 * cols * NODES, LANES), F32),
            pltpu.VMEM((blocks * ROWS, LANES), F32),
            pltpu.VMEM((blocks, ROWS, LANES), F32),
            pltpu.VMEM((3 * ROWS, blocks * LANES), BF16),
            pltpu.VMEM((extra * LANES, blocks * LANES), BF16),
            pltpu.VMEM(((blocks + extra) * LANES, LANES), F32),
            pltpu.VMEM((blocks * LANES, LANES), F32),
            pltpu.SMEM((1, 6 * width), jnp.int32),
            pltpu.SemaphoreType.DMA,
            pltpu.VMEM((5, 6 * NODES, width), BF16),
            pltpu.VMEM((5, 2 * NODES, width), BF16),
            pltpu.VMEM((ROWS, extra * LANES), F32),
            pltpu.VMEM((3 * NODES, width), F32),
            pltpu.VMEM((width, nd * LANES), BF16),
            pltpu.VMEM((6 * NODES, nd * LANES), BF16),
            pltpu.VMEM((nd, 24, LANES), F32),
            pltpu.VMEM((nd, 24, LANES), F32),
            pltpu.VMEM((nd, 16, LANES), F32),
            pltpu.VMEM((nd, 16, LANES), F32),
            pltpu.VMEM((2, 2, ROWS, LANES), F32),
            pltpu.VMEM((2, 2, ROWS, LANES), F32),
            pltpu.SemaphoreType.DMA((2, nd)),
            pltpu.SemaphoreType.DMA((2, nd)),
            pltpu.SemaphoreType.DMA((2, 2)),
            pltpu.SemaphoreType.DMA((2, 2)),
        ],
        compiler_params=pltpu.CompilerParams(
            collective_id=0, has_side_effects=True, vmem_limit_bytes=48 * 1024 * 1024
        ),
    )(
        density,
        momentum,
        energy,
        face_link.reshape(1, 6 * width),
        owner_rank,
        owner_element,
        offsets,
        forces,
        jnp.asarray(split_table(dcat)),
        jnp.asarray(split_table(filt)),
    )


def solution(mesh):
    element = P(None, ("group", "dom"))
    stacked = P(None, None, ("group", "dom"))
    return jax.shard_map(
        body,
        mesh=mesh,
        in_specs=(
            element,
            stacked,
            element,
            P("group", "dom", None),
            P(("group", "dom"), None),
            element,
            stacked,
            element,
        ),
        out_specs=(element, stacked, element, stacked),
        check_vma=False,
    )
```

```python
import functools
import math

import jax
import jax.numpy as jnp
import numpy as np
from jax import lax
from jax.experimental import pallas as pl
from jax.experimental.pallas import tpu as pltpu
from jax.sharding import PartitionSpec as P

CAP = 32
TIME_STEP = 0.005
SPREAD_WIDTH = 0.5
LIFT_FACTOR = 6.0
HEAT_RATIO = 1.4
LANES = 128
NODES = 64
ROWS = 80
MESH = pl.DeviceIdType.MESH
F32 = jnp.float32
BF16 = jnp.bfloat16


def basis_tables():
    nodes = np.array([-1.0, -math.sqrt(0.2), math.sqrt(0.2), 1.0])
    weights = np.array(
        [1.0 / np.prod([nodes[a] - nodes[c] for c in range(4) if c != a]) for a in range(4)]
    )
    deriv = np.zeros((4, 4))
    for a in range(4):
        for b in range(4):
            if a != b:
                deriv[a, b] = weights[b] / weights[a] / (nodes[a] - nodes[b])
        deriv[a, a] = -np.sum(deriv[a])
    vander = np.stack(
        [np.ones(4), nodes, 1.5 * nodes**2 - 0.5, 2.5 * nodes**3 - 1.5 * nodes], axis=1
    )
    one_dim = vander * np.array([1.0, 1.0, 1.0, 0.75])[None, :] @ np.linalg.inv(vander)
    eye = np.eye(4)
    dcat = np.concatenate(
        [
            np.kron(eye, np.kron(eye, deriv)),
            np.kron(eye, np.kron(deriv, eye)),
            np.kron(deriv, np.kron(eye, eye)),
        ],
        axis=1,
    )
    filt = np.kron(one_dim, np.kron(one_dim, one_dim))
    return nodes, dcat, filt


def split_table(table):
    table = np.asarray(table, np.float32)
    high = table.astype(BF16)
    low = (table - high.astype(np.float32)).astype(BF16)
    top = np.concatenate([high, high], axis=1)
    bottom = np.concatenate([low, np.zeros_like(low)], axis=1)
    return np.concatenate([top, bottom], axis=0)


def split2(x):
    high = x.astype(BF16)
    return high, (x - high.astype(F32)).astype(BF16)


def split3(x):
    high = x.astype(BF16)
    rest = x - high.astype(F32)
    middle = rest.astype(BF16)
    return high, middle, (rest - middle.astype(F32)).astype(BF16)


def dot_nt(a, b):
    return lax.dot_general(a, b, (((1,), (1,)), ((), ())), preferred_element_type=F32)


def pick_lanes(x, index):
    return jnp.take_along_axis(x, index, axis=1, mode="promise_in_bounds")


def state_of(rows):
    inverse = 1.0 / rows[0]
    vel = [rows[1 + c] * inverse for c in range(3)]
    press = (HEAT_RATIO - 1.0) * (
        rows[4] - 0.5 * (rows[1] * vel[0] + rows[2] * vel[1] + rows[3] * vel[2])
    )
    return inverse, vel, press


def flux_of(rows, vel, press, d):
    along = vel[d]
    out = [
        rows[1 + d],
        rows[1] * along,
        rows[2] * along,
        rows[3] * along,
        (rows[4] + press) * along,
    ]
    out[1 + d] = out[1 + d] + press
    return out


def place_kernel(den, mom, ene, tend, o_den, o_mom, o_ene, o_tend, sem):
    pairs = [(tend.at[v], o_tend.at[v]) for v in range(5)]
    pairs += [(mom.at[v], o_mom.at[v]) for v in range(3)] + [(den, o_den), (ene, o_ene)]
    moves = [
        pltpu.make_async_copy(source, target, sem.at[i])
        for i, (source, target) in enumerate(pairs)
    ]
    for move in moves:
        move.start()
    for move in moves:
        move.wait()


def kernel(
    nd, ng, nodes,
    den_in, mom_in, ene_in, link_in, rank_in, elem_in, off_in, force_in, dmat_in, fmat_in,
    to_den, to_mom, to_ene, to_tend,
    den, mom, ene, link, rank, elem, off, force, dmat, fmat, load_sem,
    o_den, o_mom, o_ene, o_tend, store_sem,
    q, q1, td, tr, nb, t3, oh, tall, got, index, index_sem, fx, xf, ex, src, ohe, ct,
    s1, r1, s2, r2, rs, rr, send_sem, recv_sem, rim_send_sem, rim_recv_sem,
):
    pairs = (
        (link_in, link), (den_in, den), (mom_in, mom), (ene_in, ene), (rank_in, rank),
        (elem_in, elem), (off_in, off), (force_in, force), (dmat_in, dmat), (fmat_in, fmat),
    )
    loads = [
        pltpu.make_async_copy(source, target, load_sem.at[i])
        for i, (source, target) in enumerate(pairs)
    ]
    for load in loads:
        load.start()
    width = den.shape[1]
    cols = width // LANES
    blocks = 6 * cols
    shared = nd * (width // 32)
    shared_blocks = shared // LANES
    extra = shared_blocks + 2
    me = lax.axis_index("dom")
    group = lax.axis_index("group")
    up, down = lax.rem(group + 1, ng), lax.rem(group + ng - 1, ng)

    fetch = pltpu.make_async_copy(link_in, index, index_sem)
    fetch.start()
    barrier = pltpu.get_barrier_semaphore()
    for d in range(1, nd):
        pl.semaphore_signal(
            barrier, inc=1, device_id={"dom": lax.rem(me + d, nd)}, device_id_type=MESH
        )
    for target in (up, down):
        pl.semaphore_signal(barrier, inc=1, device_id={"group": target}, device_id_type=MESH)

    def at(v, c):
        return (v * cols + c) * NODES

    loads[0].wait()
    row_ids = lax.broadcasted_iota(jnp.int32, (extra * LANES, LANES), 0) + 6 * width
    for b in range(blocks):
        part = link[0:1, b * LANES : (b + 1) * LANES]
        oh[:, b * LANES : (b + 1) * LANES] = jnp.where(row_ids == part, 1.0, 0.0).astype(BF16)

    for load in loads[1:]:
        load.wait()
    for c in range(cols):
        lanes = slice(c * LANES, (c + 1) * LANES)
        q[at(0, c) : at(0, c) + NODES, :] = den[:, lanes]
        for v in range(3):
            q[at(1 + v, c) : at(1 + v, c) + NODES, :] = mom[v, :, lanes]
        q[at(4, c) : at(4, c) + NODES, :] = ene[:, lanes]

    def fill_traces(ref):
        for c in range(cols):
            for v in range(5):
                base = at(v, c)
                for t in range(6):
                    dst = (t * cols + c) * ROWS + v * 16
                    if t < 2:
                        tr[dst : dst + 16, :] = ref[pl.ds(base + 3 * t, 16, 4), :]
                    elif t < 4:
                        for k in range(4):
                            first = base + 16 * k + 12 * (t - 2)
                            tr[dst + 4 * k : dst + 4 * k + 4, :] = ref[first : first + 4, :]
                    else:
                        first = base + 48 * (t - 4)
                        tr[dst : dst + 16, :] = ref[first : first + 16, :]

    def prepare(send, section):
        for b in range(blocks):
            parts = split3(tr[b * ROWS : (b + 1) * ROWS, :])
            for s in range(3):
                t3[s * ROWS : (s + 1) * ROWS, b * LANES : (b + 1) * LANES] = parts[s]
        out = dot_nt(t3[...], oh[...])
        out = out[:ROWS] + out[ROWS : 2 * ROWS] + out[2 * ROWS :]
        for j in range(shared_blocks):
            block = jnp.concatenate(
                [out[:, j * LANES : (j + 1) * LANES], jnp.zeros((LANES - ROWS, LANES), F32)], axis=0
            )
            flipped = block.T
            for p in range(8):
                send[j * 8 + p, 0:16, :] = flipped[p * 16 : (p + 1) * 16, :]
        for side in range(2):
            first = (shared_blocks + side) * LANES
            rs[section, side] = out[:, first : first + LANES]

    def copies(send, receive, section):
        made = []
        for d in range(1, nd):
            peer = lax.rem(me + d, nd)
            made.append(
                pltpu.make_async_remote_copy(
                    src_ref=send.at[peer],
                    dst_ref=receive.at[me],
                    send_sem=send_sem.at[section, d],
                    recv_sem=recv_sem.at[section, d],
                    device_id={"dom": peer},
                    device_id_type=MESH,
                )
            )
        for side, target in ((0, down), (1, up)):
            made.append(
                pltpu.make_async_remote_copy(
                    src_ref=rs.at[section, side],
                    dst_ref=rr.at[section, 1 - side],
                    send_sem=rim_send_sem.at[section, side],
                    recv_sem=rim_recv_sem.at[section, 1 - side],
                    device_id={"group": target},
                    device_id_type=MESH,
                )
            )
        return made

    def waits(send, receive, section):
        for d in range(1, nd):
            source = lax.rem(me + nd - d, nd)
            pltpu.make_async_remote_copy(
                src_ref=send.at[lax.rem(me + d, nd)],
                dst_ref=receive.at[source],
                send_sem=send_sem.at[section, d],
                recv_sem=recv_sem.at[section, d],
                device_id={"dom": lax.rem(me + d, nd)},
                device_id_type=MESH,
            ).wait()
        for side, target in ((0, down), (1, up)):
            pltpu.make_async_remote_copy(
                src_ref=rs.at[section, side],
                dst_ref=rr.at[section, side],
                send_sem=rim_send_sem.at[section, side],
                recv_sem=rim_recv_sem.at[section, side],
                device_id={"group": target},
                device_id_type=MESH,
            ).wait()

    def turn_traces():
        for b in range(blocks):
            block = jnp.concatenate(
                [tr[b * ROWS : (b + 1) * ROWS, :], jnp.zeros((LANES - ROWS, LANES), F32)], axis=0
            )
            tall[b * LANES : (b + 1) * LANES, :] = block.T

    def gather_own():
        def rows_of(ob, carry):
            for r in range(LANES):
                face = ob * LANES + r
                got[pl.ds(face, 1), :] = tall[pl.ds(index[0, face], 1), :]
            return carry

        lax.fori_loop(0, blocks, rows_of, 0)
        for b in range(blocks):
            nb[b] = got[b * LANES : (b + 1) * LANES, :].T[:ROWS]

    def unpack(receive, section):
        for j in range(shared_blocks):
            block = jnp.concatenate([receive[j * 8 + p, 0:16, :] for p in range(8)], axis=0)
            ex[:, j * LANES : (j + 1) * LANES] = block.T[:ROWS]
        for side in range(2):
            first = (shared_blocks + side) * LANES
            ex[:, first : first + LANES] = rr[section, side]

    def gather_arrived():
        parts = split2(ex[...])
        stacked = jnp.concatenate(parts, axis=0)
        out = jnp.dot(stacked, oh[...], preferred_element_type=F32)
        for b in range(blocks):
            lanes = slice(b * LANES, (b + 1) * LANES)
            nb[b] = nb[b] + (out[:ROWS, lanes] + out[ROWS:, lanes])

    def volume(ref):
        for c in range(cols):
            lanes = slice(c * LANES, (c + 1) * LANES)
            for n in range(0, NODES, 16):
                rows = [ref[at(v, c) + n : at(v, c) + n + 16, :] for v in range(5)]
                _, vel, press = state_of(rows)
                for d in range(3):
                    flux = flux_of(rows, vel, press, d)
                    for v in range(5):
                        high, low = split2(flux[v])
                        fx[v, d * NODES + n : d * NODES + n + 16, lanes] = high
                        fx[v, (3 + d) * NODES + n : (3 + d) * NODES + n + 16, lanes] = low
        for v in range(5):
            out = jnp.dot(dmat[...].astype(BF16), fx[v], preferred_element_type=F32)
            out = -(out[:NODES] + out[NODES:])
            for c in range(cols):
                td[at(v, c) : at(v, c) + NODES, :] = out[:, c * LANES : (c + 1) * LANES]

    def surface():
        for t in range(6):
            d = t // 2
            outward = 1.0 if t % 2 else -1.0
            for c in range(cols):
                b = t * cols + c
                inside = [tr[b * ROWS + v * 16 : b * ROWS + v * 16 + 16, :] for v in range(5)]
                outside = [nb[b, v * 16 : v * 16 + 16, :] for v in range(5)]
                inv_a, vel_a, press_a = state_of(inside)
                inv_b, vel_b, press_b = state_of(outside)
                lam = jnp.maximum(
                    jnp.abs(vel_a[d]) + jnp.sqrt(HEAT_RATIO * press_a * inv_a),
                    jnp.abs(vel_b[d]) + jnp.sqrt(HEAT_RATIO * press_b * inv_b),
                )
                lam = (0.5 * LIFT_FACTOR) * lam
                flux_a = flux_of(inside, vel_a, press_a, d)
                flux_b = flux_of(outside, vel_b, press_b, d)
                for v in range(5):
                    fix = lam * (outside[v] - inside[v]) - (0.5 * LIFT_FACTOR * outward) * (
                        flux_b[v] - flux_a[v]
                    )
                    base = at(v, c)
                    if t < 2:
                        place = pl.ds(base + 3 * t, 16, 4)
                        td[place, :] = td[place, :] + fix
                    elif t < 4:
                        for k in range(4):
                            first = base + 16 * k + 12 * (t - 2)
                            td[first : first + 4, :] = (
                                td[first : first + 4, :] + fix[4 * k : 4 * k + 4, :]
                            )
                    else:
                        first = base + 48 * (t - 4)
                        td[first : first + 16, :] = td[first : first + 16, :] + fix

    def finish(ref, second):
        for c in range(cols):
            lanes = slice(c * LANES, (c + 1) * LANES)
            for n in range(0, NODES, 16):
                rows = [ref[at(v, c) + n : at(v, c) + n + 16, :] for v in range(5)]
                rate = [td[at(v, c) + n : at(v, c) + n + 16, :] for v in range(5)]
                push = [src[k * NODES + n : k * NODES + n + 16, lanes] for k in range(3)]
                inverse = 1.0 / rows[0]
                work = (push[0] * rows[1] + push[1] * rows[2] + push[2] * rows[3]) * inverse
                rate = [
                    rate[0], rate[1] + push[0], rate[2] + push[1], rate[3] + push[2], rate[4] + work
                ]
                for v in range(5):
                    moved = rows[v] + TIME_STEP * rate[v]
                    if second:
                        o_tend[v, n : n + 16, lanes] = rate[v]
                        moved = 0.75 * q[at(v, c) + n : at(v, c) + n + 16, :] + 0.25 * moved
                    high, low = split2(moved)
                    xf[v, n : n + 16, lanes] = high
                    xf[v, NODES + n : NODES + n + 16, lanes] = low
        stores = []
        if second:
            stores.append(pltpu.make_async_copy(o_tend, to_tend, store_sem.at[5]))
            stores[0].start()
        targets = [
            (o_den, to_den), (o_mom.at[0], to_mom.at[0]), (o_mom.at[1], to_mom.at[1]),
            (o_mom.at[2], to_mom.at[2]), (o_ene, to_ene),
        ]
        for v in range(5):
            out = jnp.dot(fmat[...].astype(BF16), xf[v], preferred_element_type=F32)
            out = out[:NODES] + out[NODES:]
            if not second:
                for c in range(cols):
                    q1[at(v, c) : at(v, c) + NODES, :] = out[:, c * LANES : (c + 1) * LANES]
            elif v == 0:
                o_den[...] = out
            elif v == 4:
                o_ene[...] = out
            else:
                o_mom[v - 1] = out
            if second:
                stores.append(pltpu.make_async_copy(*targets[v], store_sem.at[v]))
                stores[-1].start()
        for store in stores:
            store.wait()

    def pack_points():
        across = jnp.broadcast_to(rank[...].astype(F32), (LANES, LANES))
        column = across.T
        earlier = lax.broadcasted_iota(jnp.int32, (LANES, LANES), 1) < lax.broadcasted_iota(
            jnp.int32, (LANES, LANES), 0
        )
        place = jnp.sum(
            jnp.where((column == across) & earlier, 1.0, 0.0), axis=1, keepdims=True
        )
        target = column[:, 0:1] * float(LANES) + place
        slots = lax.broadcasted_iota(jnp.int32, (LANES, nd * LANES), 1).astype(F32)
        total = None
        for k in range(4):
            spread = jnp.where(target + float(k * CAP) == slots, 1.0, 0.0).astype(BF16)
            data = jnp.concatenate(
                [elem[k : k + 1, :].astype(F32)]
                + [off[x, k : k + 1, :] for x in range(3)]
                + [force[...], jnp.zeros((1, LANES), F32)],
                axis=0,
            )
            stacked = jnp.concatenate([part.astype(F32) for part in split3(data)], axis=0)
            out = jnp.dot(stacked.astype(BF16), spread, preferred_element_type=F32)
            total = out if total is None else total + out
        total = total[:8] + total[8:16] + total[16:]
        for a in range(nd):
            s1[a, 16:24, :] = total[:, a * LANES : (a + 1) * LANES]

    def spread_sources():
        n = lax.broadcasted_iota(jnp.int32, (NODES, LANES), 0)
        places = [n & 3, (n >> 2) & 3, n >> 4]
        coords = [
            jnp.where(
                p < 2,
                jnp.where(p == 0, float(nodes[0]), float(nodes[1])),
                jnp.where(p == 2, float(nodes[2]), float(nodes[3])),
            )
            for p in places
        ]
        element_ids = lax.broadcasted_iota(jnp.int32, (width, LANES), 0).astype(F32)
        for b in range(nd):
            lanes = slice(b * LANES, (b + 1) * LANES)
            tile = r1[b, 16:24, :]
            ohe[:, lanes] = jnp.where(element_ids == tile[0:1, :], 1.0, 0.0).astype(BF16)
            gap = [coords[x] - tile[1 + x : 2 + x, :] for x in range(3)]
            distance = gap[0] * gap[0] + gap[1] * gap[1] + gap[2] * gap[2]
            weight = jnp.exp(distance * (-1.0 / SPREAD_WIDTH))
            for x in range(3):
                high, low = split2(weight * tile[4 + x : 5 + x, :])
                ct[x * NODES : (x + 1) * NODES, lanes] = high
                ct[(3 + x) * NODES : (4 + x) * NODES, lanes] = low
        out = dot_nt(ct[...], ohe[...])
        src[...] = out[: 3 * NODES] + out[3 * NODES :]

    tall[6 * width :, :] = jnp.zeros((extra * LANES, LANES), F32)
    fetch.wait()
    fill_traces(q)
    pack_points()
    prepare(s1, 0)
    pl.semaphore_wait(barrier, nd + 1)
    for copy in copies(s1, r1, 0):
        copy.start()
    r1[me] = s1[me]
    turn_traces()
    volume(q)
    gather_own()
    waits(s1, r1, 0)
    unpack(r1, 0)
    spread_sources()
    gather_arrived()
    surface()
    finish(q, False)

    fill_traces(q1)
    prepare(s2, 1)
    for copy in copies(s2, r2, 1):
        copy.start()
    r2[me] = s2[me]
    turn_traces()
    volume(q1)
    gather_own()
    waits(s2, r2, 1)
    unpack(r2, 1)
    gather_arrived()
    surface()
    finish(q1, True)


def body(density, momentum, energy, face_link, owner_rank, owner_element, offsets, forces):
    nd, ng = lax.axis_size("dom"), lax.axis_size("group")
    width = density.shape[1]
    cols = width // LANES
    blocks = 6 * cols
    extra = nd * (width // 32) // LANES + 2
    nodes, dcat, filt = basis_tables()
    points = owner_rank.shape[0]
    hbm = pl.BlockSpec(memory_space=pltpu.HBM)
    shape = jax.ShapeDtypeStruct
    results = (
        shape((NODES, width), F32),
        shape((3, NODES, width), F32),
        shape((NODES, width), F32),
        shape((5, NODES, width), F32),
    )
    held = pl.pallas_call(
        functools.partial(kernel, nd, ng, nodes),
        out_shape=results,
        in_specs=[hbm] * 10,
        out_specs=(hbm,) * 4,
        scratch_shapes=[
            pltpu.VMEM((NODES, width), F32),
            pltpu.VMEM((3, NODES, width), F32),
            pltpu.VMEM((NODES, width), F32),
            pltpu.VMEM((1, 6 * width), jnp.int32),
            pltpu.VMEM((1, points), jnp.int32),
            pltpu.VMEM((4, points), jnp.int32),
            pltpu.VMEM((3, 4, points), F32),
            pltpu.VMEM((3, points), F32),
            pltpu.VMEM((2 * NODES, 6 * NODES), F32),
            pltpu.VMEM((2 * NODES, 2 * NODES), F32),
            pltpu.SemaphoreType.DMA((10,)),
            pltpu.VMEM((NODES, width), F32),
            pltpu.VMEM((3, NODES, width), F32),
            pltpu.VMEM((NODES, width), F32),
            pltpu.VMEM((5, NODES, width), F32),
            pltpu.SemaphoreType.DMA((6,)),
            pltpu.VMEM((5 * cols * NODES, LANES), F32),
            pltpu.VMEM((5 * cols * NODES, LANES), F32),
            pltpu.VMEM((5 * cols * NODES, LANES), F32),
            pltpu.VMEM((blocks * ROWS, LANES), F32),
            pltpu.VMEM((blocks, ROWS, LANES), F32),
            pltpu.VMEM((3 * ROWS, blocks * LANES), BF16),
            pltpu.VMEM((extra * LANES, blocks * LANES), BF16),
            pltpu.VMEM(((blocks + extra) * LANES, LANES), F32),
            pltpu.VMEM((blocks * LANES, LANES), F32),
            pltpu.SMEM((1, 6 * width), jnp.int32),
            pltpu.SemaphoreType.DMA,
            pltpu.VMEM((5, 6 * NODES, width), BF16),
            pltpu.VMEM((5, 2 * NODES, width), BF16),
            pltpu.VMEM((ROWS, extra * LANES), F32),
            pltpu.VMEM((3 * NODES, width), F32),
            pltpu.VMEM((width, nd * LANES), BF16),
            pltpu.VMEM((6 * NODES, nd * LANES), BF16),
            pltpu.VMEM((nd, 24, LANES), F32),
            pltpu.VMEM((nd, 24, LANES), F32),
            pltpu.VMEM((nd, 16, LANES), F32),
            pltpu.VMEM((nd, 16, LANES), F32),
            pltpu.VMEM((2, 2, ROWS, LANES), F32),
            pltpu.VMEM((2, 2, ROWS, LANES), F32),
            pltpu.SemaphoreType.DMA((2, nd)),
            pltpu.SemaphoreType.DMA((2, nd)),
            pltpu.SemaphoreType.DMA((2, 2)),
            pltpu.SemaphoreType.DMA((2, 2)),
        ],
        compiler_params=pltpu.CompilerParams(
            collective_id=0, has_side_effects=True, vmem_limit_bytes=60 * 1024 * 1024
        ),
    )(
        density,
        momentum,
        energy,
        face_link.reshape(1, 6 * width),
        owner_rank.reshape(1, points),
        owner_element,
        offsets,
        forces,
        jnp.asarray(split_table(dcat).astype(np.float32)),
        jnp.asarray(split_table(filt).astype(np.float32)),
    )
    return pl.pallas_call(
        place_kernel,
        out_shape=results,
        in_specs=[hbm] * 4,
        out_specs=(hbm,) * 4,
        scratch_shapes=[pltpu.SemaphoreType.DMA((10,))],
        compiler_params=pltpu.CompilerParams(vmem_limit_bytes=60 * 1024 * 1024),
    )(*held)


def solution(mesh):
    element = P(None, ("group", "dom"))
    stacked = P(None, None, ("group", "dom"))
    return jax.shard_map(
        body,
        mesh=mesh,
        in_specs=(
            element,
            stacked,
            element,
            P("group", "dom", None),
            P(("group", "dom"), None),
            element,
            stacked,
            element,
        ),
        out_specs=(element, stacked, element, stacked),
        check_vma=False,
    )
```

```python
import functools
import math

import jax
import jax.numpy as jnp
import numpy as np
from jax import lax
from jax.experimental import pallas as pl
from jax.experimental.pallas import tpu as pltpu
from jax.sharding import PartitionSpec as P

CAP = 32
TIME_STEP = 0.005
SPREAD_WIDTH = 0.5
LIFT_FACTOR = 6.0
HEAT_RATIO = 1.4
LANES = 128
NODES = 64
ROWS = 80
MESH = pl.DeviceIdType.MESH
F32 = jnp.float32
BF16 = jnp.bfloat16


def basis_tables():
    nodes = np.array([-1.0, -math.sqrt(0.2), math.sqrt(0.2), 1.0])
    weights = np.array(
        [1.0 / np.prod([nodes[a] - nodes[c] for c in range(4) if c != a]) for a in range(4)]
    )
    deriv = np.zeros((4, 4))
    for a in range(4):
        for b in range(4):
            if a != b:
                deriv[a, b] = weights[b] / weights[a] / (nodes[a] - nodes[b])
        deriv[a, a] = -np.sum(deriv[a])
    vander = np.stack(
        [np.ones(4), nodes, 1.5 * nodes**2 - 0.5, 2.5 * nodes**3 - 1.5 * nodes], axis=1
    )
    one_dim = vander * np.array([1.0, 1.0, 1.0, 0.75])[None, :] @ np.linalg.inv(vander)
    eye = np.eye(4)
    dcat = np.concatenate(
        [
            np.kron(eye, np.kron(eye, deriv)),
            np.kron(eye, np.kron(deriv, eye)),
            np.kron(deriv, np.kron(eye, eye)),
        ],
        axis=1,
    )
    filt = np.kron(one_dim, np.kron(one_dim, one_dim))
    return nodes, dcat, filt


def split_table(table):
    table = np.asarray(table, np.float32)
    high = table.astype(BF16)
    low = (table - high.astype(np.float32)).astype(BF16)
    top = np.concatenate([high, high], axis=1)
    bottom = np.concatenate([low, np.zeros_like(low)], axis=1)
    return np.concatenate([top, bottom], axis=0)


def split2(x):
    high = x.astype(BF16)
    return high, (x - high.astype(F32)).astype(BF16)


def split3(x):
    high = x.astype(BF16)
    rest = x - high.astype(F32)
    middle = rest.astype(BF16)
    return high, middle, (rest - middle.astype(F32)).astype(BF16)


def dot_nt(a, b):
    return lax.dot_general(a, b, (((1,), (1,)), ((), ())), preferred_element_type=F32)


def pick_lanes(x, index):
    return jnp.take_along_axis(x, index, axis=1, mode="promise_in_bounds")


def state_of(rows):
    inverse = 1.0 / rows[0]
    vel = [rows[1 + c] * inverse for c in range(3)]
    press = (HEAT_RATIO - 1.0) * (
        rows[4] - 0.5 * (rows[1] * vel[0] + rows[2] * vel[1] + rows[3] * vel[2])
    )
    return inverse, vel, press


def flux_of(rows, vel, press, d):
    along = vel[d]
    out = [
        rows[1 + d],
        rows[1] * along,
        rows[2] * along,
        rows[3] * along,
        (rows[4] + press) * along,
    ]
    out[1 + d] = out[1 + d] + press
    return out


def place_kernel(den, mom, ene, tend, o_den, o_mom, o_ene, o_tend, held, load_sem, store_sem):
    pairs = [(tend.at[v], o_tend.at[v]) for v in range(5)]
    pairs += [(mom.at[v], o_mom.at[v]) for v in range(3)] + [(den, o_den), (ene, o_ene)]
    loads = [
        pltpu.make_async_copy(pair[0], held.at[i], load_sem.at[i]) for i, pair in enumerate(pairs)
    ]
    stores = [
        pltpu.make_async_copy(held.at[i], pair[1], store_sem.at[i]) for i, pair in enumerate(pairs)
    ]
    for load in loads:
        load.start()
    for load, store in zip(loads, stores):
        load.wait()
        store.start()
    for store in stores:
        store.wait()


def kernel(
    nd, ng, nodes,
    den_in, mom_in, ene_in, link_in, rank_in, elem_in, off_in, force_in, dmat_in, fmat_in,
    to_den, to_mom, to_ene, to_tend,
    den, mom, ene, link, rank, elem, off, force, dmat, fmat, load_sem,
    o_den, o_mom, o_ene, o_tend, store_sem,
    q, q1, td, tr, nb, t3, oh, tall, got, index, index_sem, fx, xf, ex, src, ohe, ct,
    s1, r1, s2, r2, rs, rr, send_sem, recv_sem, rim_send_sem, rim_recv_sem,
):
    pairs = (
        (link_in, link), (den_in, den), (mom_in, mom), (ene_in, ene), (rank_in, rank),
        (elem_in, elem), (off_in, off), (force_in, force), (dmat_in, dmat), (fmat_in, fmat),
    )
    loads = [
        pltpu.make_async_copy(source, target, load_sem.at[i])
        for i, (source, target) in enumerate(pairs)
    ]
    for load in loads:
        load.start()
    width = den.shape[1]
    cols = width // LANES
    blocks = 6 * cols
    shared = nd * (width // 32)
    shared_blocks = shared // LANES
    extra = shared_blocks + 2
    me = lax.axis_index("dom")
    group = lax.axis_index("group")
    up, down = lax.rem(group + 1, ng), lax.rem(group + ng - 1, ng)

    fetch = pltpu.make_async_copy(link_in, index, index_sem)
    fetch.start()
    barrier = pltpu.get_barrier_semaphore()
    for d in range(1, nd):
        pl.semaphore_signal(
            barrier, inc=1, device_id={"dom": lax.rem(me + d, nd)}, device_id_type=MESH
        )
    for target in (up, down):
        pl.semaphore_signal(barrier, inc=1, device_id={"group": target}, device_id_type=MESH)

    def at(v, c):
        return (v * cols + c) * NODES

    loads[0].wait()
    row_ids = lax.broadcasted_iota(jnp.int32, (extra * LANES, LANES), 0) + 6 * width
    for b in range(blocks):
        part = link[0:1, b * LANES : (b + 1) * LANES]
        oh[:, b * LANES : (b + 1) * LANES] = jnp.where(row_ids == part, 1.0, 0.0).astype(BF16)

    for load in loads[1:]:
        load.wait()
    for c in range(cols):
        lanes = slice(c * LANES, (c + 1) * LANES)
        q[at(0, c) : at(0, c) + NODES, :] = den[:, lanes]
        for v in range(3):
            q[at(1 + v, c) : at(1 + v, c) + NODES, :] = mom[v, :, lanes]
        q[at(4, c) : at(4, c) + NODES, :] = ene[:, lanes]

    def fill_traces(ref):
        for c in range(cols):
            for v in range(5):
                base = at(v, c)
                for t in range(6):
                    dst = (t * cols + c) * ROWS + v * 16
                    if t < 2:
                        tr[dst : dst + 16, :] = ref[pl.ds(base + 3 * t, 16, 4), :]
                    elif t < 4:
                        for k in range(4):
                            first = base + 16 * k + 12 * (t - 2)
                            tr[dst + 4 * k : dst + 4 * k + 4, :] = ref[first : first + 4, :]
                    else:
                        first = base + 48 * (t - 4)
                        tr[dst : dst + 16, :] = ref[first : first + 16, :]

    def prepare(send, section):
        for b in range(blocks):
            parts = split3(tr[b * ROWS : (b + 1) * ROWS, :])
            for s in range(3):
                t3[s * ROWS : (s + 1) * ROWS, b * LANES : (b + 1) * LANES] = parts[s]
        out = dot_nt(t3[...], oh[...])
        out = out[:ROWS] + out[ROWS : 2 * ROWS] + out[2 * ROWS :]
        for j in range(shared_blocks):
            block = jnp.concatenate(
                [out[:, j * LANES : (j + 1) * LANES], jnp.zeros((LANES - ROWS, LANES), F32)], axis=0
            )
            flipped = block.T
            for p in range(8):
                send[j * 8 + p, 0:16, :] = flipped[p * 16 : (p + 1) * 16, :]
        for side in range(2):
            first = (shared_blocks + side) * LANES
            rs[section, side] = out[:, first : first + LANES]

    def copies(send, receive, section):
        made = []
        for d in range(1, nd):
            peer = lax.rem(me + d, nd)
            made.append(
                pltpu.make_async_remote_copy(
                    src_ref=send.at[peer],
                    dst_ref=receive.at[me],
                    send_sem=send_sem.at[section, d],
                    recv_sem=recv_sem.at[section, d],
                    device_id={"dom": peer},
                    device_id_type=MESH,
                )
            )
        for side, target in ((0, down), (1, up)):
            made.append(
                pltpu.make_async_remote_copy(
                    src_ref=rs.at[section, side],
                    dst_ref=rr.at[section, 1 - side],
                    send_sem=rim_send_sem.at[section, side],
                    recv_sem=rim_recv_sem.at[section, 1 - side],
                    device_id={"group": target},
                    device_id_type=MESH,
                )
            )
        return made

    def waits(send, receive, section):
        for d in range(1, nd):
            source = lax.rem(me + nd - d, nd)
            pltpu.make_async_remote_copy(
                src_ref=send.at[lax.rem(me + d, nd)],
                dst_ref=receive.at[source],
                send_sem=send_sem.at[section, d],
                recv_sem=recv_sem.at[section, d],
                device_id={"dom": lax.rem(me + d, nd)},
                device_id_type=MESH,
            ).wait()
        for side, target in ((0, down), (1, up)):
            pltpu.make_async_remote_copy(
                src_ref=rs.at[section, side],
                dst_ref=rr.at[section, side],
                send_sem=rim_send_sem.at[section, side],
                recv_sem=rim_recv_sem.at[section, side],
                device_id={"group": target},
                device_id_type=MESH,
            ).wait()

    def turn_traces():
        for b in range(blocks):
            block = jnp.concatenate(
                [tr[b * ROWS : (b + 1) * ROWS, :], jnp.zeros((LANES - ROWS, LANES), F32)], axis=0
            )
            tall[b * LANES : (b + 1) * LANES, :] = block.T

    def gather_own():
        def rows_of(ob, carry):
            for r in range(LANES):
                face = ob * LANES + r
                got[pl.ds(face, 1), :] = tall[pl.ds(index[0, face], 1), :]
            return carry

        lax.fori_loop(0, blocks, rows_of, 0)
        for b in range(blocks):
            nb[b] = got[b * LANES : (b + 1) * LANES, :].T[:ROWS]

    def unpack(receive, section):
        for j in range(shared_blocks):
            block = jnp.concatenate([receive[j * 8 + p, 0:16, :] for p in range(8)], axis=0)
            ex[:, j * LANES : (j + 1) * LANES] = block.T[:ROWS]
        for side in range(2):
            first = (shared_blocks + side) * LANES
            ex[:, first : first + LANES] = rr[section, side]

    def gather_arrived():
        parts = split2(ex[...])
        stacked = jnp.concatenate(parts, axis=0)
        out = jnp.dot(stacked, oh[...], preferred_element_type=F32)
        for b in range(blocks):
            lanes = slice(b * LANES, (b + 1) * LANES)
            nb[b] = nb[b] + (out[:ROWS, lanes] + out[ROWS:, lanes])

    def volume(ref):
        for c in range(cols):
            lanes = slice(c * LANES, (c + 1) * LANES)
            for n in range(0, NODES, 16):
                rows = [ref[at(v, c) + n : at(v, c) + n + 16, :] for v in range(5)]
                _, vel, press = state_of(rows)
                for d in range(3):
                    flux = flux_of(rows, vel, press, d)
                    for v in range(5):
                        high, low = split2(flux[v])
                        fx[v, d * NODES + n : d * NODES + n + 16, lanes] = high
                        fx[v, (3 + d) * NODES + n : (3 + d) * NODES + n + 16, lanes] = low
        for v in range(5):
            out = jnp.dot(dmat[...].astype(BF16), fx[v], preferred_element_type=F32)
            out = -(out[:NODES] + out[NODES:])
            for c in range(cols):
                td[at(v, c) : at(v, c) + NODES, :] = out[:, c * LANES : (c + 1) * LANES]

    def surface():
        for t in range(6):
            d = t // 2
            outward = 1.0 if t % 2 else -1.0
            for c in range(cols):
                b = t * cols + c
                inside = [tr[b * ROWS + v * 16 : b * ROWS + v * 16 + 16, :] for v in range(5)]
                outside = [nb[b, v * 16 : v * 16 + 16, :] for v in range(5)]
                inv_a, vel_a, press_a = state_of(inside)
                inv_b, vel_b, press_b = state_of(outside)
                lam = jnp.maximum(
                    jnp.abs(vel_a[d]) + jnp.sqrt(HEAT_RATIO * press_a * inv_a),
                    jnp.abs(vel_b[d]) + jnp.sqrt(HEAT_RATIO * press_b * inv_b),
                )
                lam = (0.5 * LIFT_FACTOR) * lam
                flux_a = flux_of(inside, vel_a, press_a, d)
                flux_b = flux_of(outside, vel_b, press_b, d)
                for v in range(5):
                    fix = lam * (outside[v] - inside[v]) - (0.5 * LIFT_FACTOR * outward) * (
                        flux_b[v] - flux_a[v]
                    )
                    base = at(v, c)
                    if t < 2:
                        place = pl.ds(base + 3 * t, 16, 4)
                        td[place, :] = td[place, :] + fix
                    elif t < 4:
                        for k in range(4):
                            first = base + 16 * k + 12 * (t - 2)
                            td[first : first + 4, :] = (
                                td[first : first + 4, :] + fix[4 * k : 4 * k + 4, :]
                            )
                    else:
                        first = base + 48 * (t - 4)
                        td[first : first + 16, :] = td[first : first + 16, :] + fix

    def finish(ref, second):
        for c in range(cols):
            lanes = slice(c * LANES, (c + 1) * LANES)
            for n in range(0, NODES, 16):
                rows = [ref[at(v, c) + n : at(v, c) + n + 16, :] for v in range(5)]
                rate = [td[at(v, c) + n : at(v, c) + n + 16, :] for v in range(5)]
                push = [src[k * NODES + n : k * NODES + n + 16, lanes] for k in range(3)]
                inverse = 1.0 / rows[0]
                work = (push[0] * rows[1] + push[1] * rows[2] + push[2] * rows[3]) * inverse
                rate = [
                    rate[0], rate[1] + push[0], rate[2] + push[1], rate[3] + push[2], rate[4] + work
                ]
                for v in range(5):
                    moved = rows[v] + TIME_STEP * rate[v]
                    if second:
                        o_tend[v, n : n + 16, lanes] = rate[v]
                        moved = 0.75 * q[at(v, c) + n : at(v, c) + n + 16, :] + 0.25 * moved
                    high, low = split2(moved)
                    xf[v, n : n + 16, lanes] = high
                    xf[v, NODES + n : NODES + n + 16, lanes] = low
        stores = []
        if second:
            stores.append(pltpu.make_async_copy(o_tend, to_tend, store_sem.at[5]))
            stores[0].start()
        targets = [
            (o_den, to_den), (o_mom.at[0], to_mom.at[0]), (o_mom.at[1], to_mom.at[1]),
            (o_mom.at[2], to_mom.at[2]), (o_ene, to_ene),
        ]
        for v in range(5):
            out = jnp.dot(fmat[...].astype(BF16), xf[v], preferred_element_type=F32)
            out = out[:NODES] + out[NODES:]
            if not second:
                for c in range(cols):
                    q1[at(v, c) : at(v, c) + NODES, :] = out[:, c * LANES : (c + 1) * LANES]
            elif v == 0:
                o_den[...] = out
            elif v == 4:
                o_ene[...] = out
            else:
                o_mom[v - 1] = out
            if second:
                stores.append(pltpu.make_async_copy(*targets[v], store_sem.at[v]))
                stores[-1].start()
        for store in stores:
            store.wait()

    def pack_points():
        across = jnp.broadcast_to(rank[...].astype(F32), (LANES, LANES))
        column = across.T
        earlier = lax.broadcasted_iota(jnp.int32, (LANES, LANES), 1) < lax.broadcasted_iota(
            jnp.int32, (LANES, LANES), 0
        )
        place = jnp.sum(
            jnp.where((column == across) & earlier, 1.0, 0.0), axis=1, keepdims=True
        )
        target = column[:, 0:1] * float(LANES) + place
        slots = lax.broadcasted_iota(jnp.int32, (LANES, nd * LANES), 1).astype(F32)
        total = None
        for k in range(4):
            spread = jnp.where(target + float(k * CAP) == slots, 1.0, 0.0).astype(BF16)
            data = jnp.concatenate(
                [elem[k : k + 1, :].astype(F32)]
                + [off[x, k : k + 1, :] for x in range(3)]
                + [force[...], jnp.zeros((1, LANES), F32)],
                axis=0,
            )
            stacked = jnp.concatenate([part.astype(F32) for part in split3(data)], axis=0)
            out = jnp.dot(stacked.astype(BF16), spread, preferred_element_type=F32)
            total = out if total is None else total + out
        total = total[:8] + total[8:16] + total[16:]
        for a in range(nd):
            s1[a, 16:24, :] = total[:, a * LANES : (a + 1) * LANES]

    def spread_sources():
        n = lax.broadcasted_iota(jnp.int32, (NODES, LANES), 0)
        places = [n & 3, (n >> 2) & 3, n >> 4]
        coords = [
            jnp.where(
                p < 2,
                jnp.where(p == 0, float(nodes[0]), float(nodes[1])),
                jnp.where(p == 2, float(nodes[2]), float(nodes[3])),
            )
            for p in places
        ]
        element_ids = lax.broadcasted_iota(jnp.int32, (width, LANES), 0).astype(F32)
        for b in range(nd):
            lanes = slice(b * LANES, (b + 1) * LANES)
            tile = r1[b, 16:24, :]
            ohe[:, lanes] = jnp.where(element_ids == tile[0:1, :], 1.0, 0.0).astype(BF16)
            gap = [coords[x] - tile[1 + x : 2 + x, :] for x in range(3)]
            distance = gap[0] * gap[0] + gap[1] * gap[1] + gap[2] * gap[2]
            weight = jnp.exp(distance * (-1.0 / SPREAD_WIDTH))
            for x in range(3):
                high, low = split2(weight * tile[4 + x : 5 + x, :])
                ct[x * NODES : (x + 1) * NODES, lanes] = high
                ct[(3 + x) * NODES : (4 + x) * NODES, lanes] = low
        out = dot_nt(ct[...], ohe[...])
        src[...] = out[: 3 * NODES] + out[3 * NODES :]

    tall[6 * width :, :] = jnp.zeros((extra * LANES, LANES), F32)
    fetch.wait()
    fill_traces(q)
    pack_points()
    prepare(s1, 0)
    pl.semaphore_wait(barrier, nd + 1)
    for copy in copies(s1, r1, 0):
        copy.start()
    r1[me] = s1[me]
    turn_traces()
    volume(q)
    gather_own()
    waits(s1, r1, 0)
    unpack(r1, 0)
    spread_sources()
    gather_arrived()
    surface()
    finish(q, False)

    fill_traces(q1)
    prepare(s2, 1)
    for copy in copies(s2, r2, 1):
        copy.start()
    r2[me] = s2[me]
    turn_traces()
    volume(q1)
    gather_own()
    waits(s2, r2, 1)
    unpack(r2, 1)
    gather_arrived()
    surface()
    finish(q1, True)


def body(density, momentum, energy, face_link, owner_rank, owner_element, offsets, forces):
    nd, ng = lax.axis_size("dom"), lax.axis_size("group")
    width = density.shape[1]
    cols = width // LANES
    blocks = 6 * cols
    extra = nd * (width // 32) // LANES + 2
    nodes, dcat, filt = basis_tables()
    points = owner_rank.shape[0]
    hbm = pl.BlockSpec(memory_space=pltpu.HBM)
    shape = jax.ShapeDtypeStruct
    results = (
        shape((NODES, width), F32),
        shape((3, NODES, width), F32),
        shape((NODES, width), F32),
        shape((5, NODES, width), F32),
    )
    held = pl.pallas_call(
        functools.partial(kernel, nd, ng, nodes),
        out_shape=results,
        in_specs=[hbm] * 10,
        out_specs=(hbm,) * 4,
        scratch_shapes=[
            pltpu.VMEM((NODES, width), F32),
            pltpu.VMEM((3, NODES, width), F32),
            pltpu.VMEM((NODES, width), F32),
            pltpu.VMEM((1, 6 * width), jnp.int32),
            pltpu.VMEM((1, points), jnp.int32),
            pltpu.VMEM((4, points), jnp.int32),
            pltpu.VMEM((3, 4, points), F32),
            pltpu.VMEM((3, points), F32),
            pltpu.VMEM((2 * NODES, 6 * NODES), F32),
            pltpu.VMEM((2 * NODES, 2 * NODES), F32),
            pltpu.SemaphoreType.DMA((10,)),
            pltpu.VMEM((NODES, width), F32),
            pltpu.VMEM((3, NODES, width), F32),
            pltpu.VMEM((NODES, width), F32),
            pltpu.VMEM((5, NODES, width), F32),
            pltpu.SemaphoreType.DMA((6,)),
            pltpu.VMEM((5 * cols * NODES, LANES), F32),
            pltpu.VMEM((5 * cols * NODES, LANES), F32),
            pltpu.VMEM((5 * cols * NODES, LANES), F32),
            pltpu.VMEM((blocks * ROWS, LANES), F32),
            pltpu.VMEM((blocks, ROWS, LANES), F32),
            pltpu.VMEM((3 * ROWS, blocks * LANES), BF16),
            pltpu.VMEM((extra * LANES, blocks * LANES), BF16),
            pltpu.VMEM(((blocks + extra) * LANES, LANES), F32),
            pltpu.VMEM((blocks * LANES, LANES), F32),
            pltpu.SMEM((1, 6 * width), jnp.int32),
            pltpu.SemaphoreType.DMA,
            pltpu.VMEM((5, 6 * NODES, width), BF16),
            pltpu.VMEM((5, 2 * NODES, width), BF16),
            pltpu.VMEM((ROWS, extra * LANES), F32),
            pltpu.VMEM((3 * NODES, width), F32),
            pltpu.VMEM((width, nd * LANES), BF16),
            pltpu.VMEM((6 * NODES, nd * LANES), BF16),
            pltpu.VMEM((nd, 24, LANES), F32),
            pltpu.VMEM((nd, 24, LANES), F32),
            pltpu.VMEM((nd, 16, LANES), F32),
            pltpu.VMEM((nd, 16, LANES), F32),
            pltpu.VMEM((2, 2, ROWS, LANES), F32),
            pltpu.VMEM((2, 2, ROWS, LANES), F32),
            pltpu.SemaphoreType.DMA((2, nd)),
            pltpu.SemaphoreType.DMA((2, nd)),
            pltpu.SemaphoreType.DMA((2, 2)),
            pltpu.SemaphoreType.DMA((2, 2)),
        ],
        compiler_params=pltpu.CompilerParams(
            collective_id=0, has_side_effects=True, vmem_limit_bytes=60 * 1024 * 1024
        ),
    )(
        density,
        momentum,
        energy,
        face_link.reshape(1, 6 * width),
        owner_rank.reshape(1, points),
        owner_element,
        offsets,
        forces,
        jnp.asarray(split_table(dcat).astype(np.float32)),
        jnp.asarray(split_table(filt).astype(np.float32)),
    )
    return pl.pallas_call(
        place_kernel,
        out_shape=results,
        in_specs=[hbm] * 4,
        out_specs=(hbm,) * 4,
        scratch_shapes=[
            pltpu.VMEM((10, NODES, width), F32),
            pltpu.SemaphoreType.DMA((10,)),
            pltpu.SemaphoreType.DMA((10,)),
        ],
        compiler_params=pltpu.CompilerParams(vmem_limit_bytes=60 * 1024 * 1024),
    )(*held)


def solution(mesh):
    element = P(None, ("group", "dom"))
    stacked = P(None, None, ("group", "dom"))
    return jax.shard_map(
        body,
        mesh=mesh,
        in_specs=(
            element,
            stacked,
            element,
            P("group", "dom", None),
            P(("group", "dom"), None),
            element,
            stacked,
            element,
        ),
        out_specs=(element, stacked, element, stacked),
        check_vma=False,
    )
```
